256 devices in a mesh: attn: 4 (over x), exp: 32 (over z, y), rep: 2 (over core).
Axes of the slice: x: 4, y: 4, z: 8, core: 2. Of those that a mesh axis runs over, the one named last changes fastest.
Arguments:
- tokens: bfloat16 [1536, 7168], P(('attn', 'exp'), 'rep'), may hold values from -6 to 6
- routes: int32 [1536, 8], P(('attn', 'exp')), may hold values from 0 to 31, all different within a row; in each aligned block of 12 rows (0 to 11, 12 to 23, ...) at most 6 rows name the same one
- route_weights: float32 [1536, 8], P(('attn', 'exp')), may hold values from 0.2 to 1.5
- w_gate: bfloat16 [32, 7168, 2048], P('exp', None, ('attn', 'rep')), may hold values from -0.0625 to 0.0625
- w_up: bfloat16 [32, 7168, 2048], P('exp', None, ('attn', 'rep')), may hold values from -0.0625 to 0.0625
- w_down: bfloat16 [32, 2048, 7168], P('exp', ('attn', 'rep')), may hold values from -0.125 to 0.125
Outputs:
- mixed: bfloat16 [1536, 7168], P(('attn', 'exp'), 'rep')
The draws below stay inside these ranges and needn't reach their ends.
Inputs may be any that keep to these rules, and one draw needn't show every extreme that they name: `routes`: the 8 experts of one request are distinct. Among the rows of one device no expert is chosen more than 6 times, and in some device some expert is chosen exactly 6 times.
All inputs are finite; a program needn't handle non-finite values.
Results may differ from the reference program's by a relative error of at most 0.02.
Values may be sent and summed in bfloat16 or wider, within the bound.
A program may use at most 128 MiB of HBM per device.

```python
import math
import jax
import jax.numpy as jnp
import numpy as np
from jax import lax

D = 7168
FF = 2048
TOPK = 8
TOK_DEV = 12
EXPERTS = 32
CAP = 6
TOKENS = 1536
N_ATTN = 4
N_REP = 2


def steps_of(own_key, extent, shards, smallest, largest):
    gain = 1.0
    for dim, blocks in shards:
        steps = jax.random.uniform(jax.random.fold_in(jax.random.fold_in(own_key, 6), dim), (blocks,), jnp.float32, smallest / len(shards), largest / len(shards))
        gain = gain * jnp.repeat(jnp.exp(steps), extent[dim] // blocks).reshape((-1,) + (1,) * (len(extent) - 1 - dim))
    return gain


def routed_block(key, own, number, rows, number_of, top, most, slope):
    ranking = jax.random.permutation(key, number_of)
    crowded, usual = portions_of(number_of, rows * top, most, slope, True), portions_of(number_of, rows * top, most, slope, False)
    places = jnp.arange(number_of)

    def named(sizes, offset_by):
        used = int((sizes > 0).sum())
        fixed = max(1, used // 4)
        passed = fixed + (places - fixed + offset_by * (used - fixed)) % max(1, number_of - fixed)
        return jnp.zeros((number_of,), jnp.int32).at[ranking[jnp.where(places < fixed, places, passed)]].set(jnp.asarray(sizes, jnp.int32))

    sizes = jnp.where(number % 4 == 0, named(crowded, number // 4), named(usual, number - number // 4 - 1))
    mixed = jax.random.permutation(jax.random.fold_in(own, 3), number_of)
    giver, receiver = mixed[0:number_of // 2 * 2:2], mixed[1:number_of // 2 * 2:2]
    slack = jnp.minimum(sizes[giver] - 1, most - sizes[receiver]) // 2
    slack = jnp.where((giver == ranking[0]) | (receiver == ranking[0]) | (sizes[receiver] == 0), 0, jnp.maximum(slack, 0))
    passed = jax.random.randint(jax.random.fold_in(own, 4), (number_of // 2,), 0, 1 << 20) % (slack + 1)
    sizes = sizes.at[giver].add(-passed).at[receiver].add(passed)
    labels = jnp.searchsorted(jnp.cumsum(sizes), jnp.arange(rows * top), side="right").astype(jnp.int32)
    grid = labels.reshape(top, rows).T
    grid = grid[jax.random.permutation(jax.random.fold_in(own, 1), rows)]
    offset_by = jax.random.randint(jax.random.fold_in(own, 2), (rows, 1), 0, top)
    return jnp.take_along_axis(grid, (jnp.arange(top)[None, :] + offset_by) % top, axis=1)


def portions_of(amount, total, bound, skew, full):
    loads = [(1 << 20) // math.isqrt(grade ** skew) + 1 for grade in range(1, amount + 1)]
    largest = bound if full else min(bound, max(-(-total // amount), total * loads[0] // sum(loads)))
    least = 1 if total - largest >= amount - 1 else 0
    holding, rest = [largest] + [least] * (amount - 1), total - largest - least * (amount - 1)
    while rest > 0:
        movable = [i for i in range(1, amount) if holding[i] < largest] or [i for i in range(1, amount) if holding[i] < bound]
        pool, budget = sum([loads[i] for i in movable]), rest
        for i in movable:
            addition = min(bound - holding[i], max(1, budget * loads[i] // pool), rest)
            holding[i] = holding[i] + addition
            rest = rest - addition
    return np.array(holding)


def centred(stream_key, shape, width, bound, split=(), kind=jnp.bfloat16):
    values = width * jax.random.normal(stream_key, shape, jnp.float32)
    if split:
        values = values * steps_of(stream_key, shape, split, -0.22, 0.18)
    return jnp.clip(values, -bound, bound).astype(kind)


def setup_inputs(seed: int = 0) -> dict:
    seeds = jax.random.split(jax.random.key(seed), 7)
    tokens = centred(seeds[0], (TOKENS, D), 1.0, 6.0, ((0, 128), (1, 2)))
    routes_keys = jax.random.split(jax.random.fold_in(seeds[1], 1), TOKENS // TOK_DEV)
    routes_turns = jax.random.permutation(jax.random.fold_in(seeds[1], 3), TOKENS // TOK_DEV)
    routes = jax.vmap(lambda own, number: routed_block(jax.random.fold_in(seeds[1], 2), own, number, TOK_DEV, EXPERTS, TOPK, CAP, 2))(routes_keys, routes_turns).reshape((TOKENS, TOPK))
    route_weights = jnp.clip(0.2 + 1.3 * jax.random.uniform(seeds[2], (TOKENS, TOPK), jnp.float32) ** steps_of(seeds[2], (TOKENS, TOPK), ((0, 128),), -0.2, 0.2), 0.2, 1.5)
    w_gate = centred(seeds[3], (EXPERTS, D, FF), D ** -0.5, 0.0625, ((0, 32), (2, 8)))
    w_up = centred(seeds[4], (EXPERTS, D, FF), D ** -0.5, 0.0625, ((0, 32), (2, 8)))
    w_down = centred(seeds[5], (EXPERTS, FF, D), FF ** -0.5, 0.125, ((0, 32), (1, 8)))
    return {"tokens": tokens, "routes": routes, "route_weights": route_weights, "w_gate": w_gate, "w_up": w_up, "w_down": w_down}


def reference(tokens, routes, route_weights, w_gate, w_up, w_down):
    blocks = TOKENS // TOK_DEV
    pairs = TOK_DEV * TOPK
    flat = routes.reshape(blocks, pairs)
    onehot = (flat[:, :, None] == jnp.arange(EXPERTS, dtype=jnp.int32)[None, None, :]).astype(jnp.int32)
    earlier = jnp.cumsum(onehot, axis=1) - onehot
    slot = jnp.sum(onehot * earlier, axis=2).astype(jnp.int32)
    stride = blocks * CAP
    position = flat * stride + jnp.arange(blocks, dtype=jnp.int32)[:, None] * CAP + slot
    position = position.reshape(-1).astype(jnp.int32)
    owner = (jnp.arange(TOKENS * TOPK, dtype=jnp.int32) // TOPK).astype(jnp.int32)
    buffer = jnp.zeros((EXPERTS * stride, D), jnp.bfloat16).at[position].set(tokens[owner])
    buffer = buffer.reshape(EXPERTS, stride, D)
    pieces = N_ATTN * N_REP
    piece_width = FF // pieces

    def expert(operands):
        rows, gate_w, up_w, down_w = operands
        gate = jnp.dot(rows, gate_w, preferred_element_type=jnp.float32)
        up = jnp.dot(rows, up_w, preferred_element_type=jnp.float32)
        hidden = (jax.nn.silu(gate) * up).astype(jnp.bfloat16)
        total = jnp.zeros((rows.shape[0], D), jnp.float32)
        for block in range(pieces):
            lower = block * piece_width
            partial_value = jnp.dot(hidden[:, lower:lower + piece_width], down_w[lower:lower + piece_width], preferred_element_type=jnp.float32).astype(jnp.bfloat16)
            partial_value = lax.optimization_barrier(partial_value)
            total = total + partial_value.astype(jnp.float32)
        return total.astype(jnp.bfloat16)

    outputs = lax.map(expert, (buffer, w_gate, w_up, w_down))
    picked = outputs.reshape(EXPERTS * stride, D)[position].astype(jnp.float32).reshape(TOKENS, TOPK, D)
    mixed = jnp.sum(picked * route_weights[:, :, None], axis=1)
    return mixed.astype(jnp.bfloat16)
```

```python
import functools

import jax
import jax.numpy as jnp
from jax import lax
from jax.experimental import pallas as pl
from jax.experimental.pallas import tpu as pltpu
from jax.sharding import PartitionSpec as P

MESH = pl.DeviceIdType.MESH
NX, NZ, NY = 4, 8, 4
NF = 4
TOK, PAD, TOP, CAP, HID = 12, 16, 8, 6, 256
COLS = 256
ROWS = NZ * CAP
PLANE = NY * ROWS
F32, BF16 = jnp.float32, jnp.bfloat16


def mm(a, b, dims=((1,), (0,))):
    return lax.dot_general(a, b, (dims, ((), ())), preferred_element_type=F32)


def iota(shape, dim):
    return lax.broadcasted_iota(jnp.int32, shape, dim)


def sixth(n):
    return (n * 10923) >> 16


def kernel(
    tokens, routes, weights, wg_hbm, wu_hbm, wd_hbm, out,
    tok, tm, pick, mix, ysend, rows, wg, wu, wd, acc, hid,
    part, sib, xback, yback, zpart, zfar, znear, opp,
    wsem, ssem, rsem,
):
    half = tokens.shape[1]
    fw = half // NF
    x = lax.axis_index("attn")
    e = lax.axis_index("exp")
    c = lax.axis_index("rep")
    z, y = e // NY, lax.rem(e, NY)
    other = 1 - c

    def dev(dx=0, dz=0, dy=0, dc=0):
        return (
            lax.rem(x + dx + NX, NX),
            lax.rem(z + dz + NZ, NZ) * NY + lax.rem(y + dy + NY, NY),
            lax.rem(c + dc, 2),
        )

    partners = [dev(dx=1), dev(dx=-1), dev(dx=2), dev(dc=1)]
    partners += [dev(dy=d) for d in (1, 2, 3)]
    partners += [dev(dz=d) for d in (1, -1, 2, -2)]
    barrier = pltpu.get_barrier_semaphore()
    for partner in partners:
        pl.semaphore_signal(barrier, inc=1, device_id=partner, device_id_type=MESH)

    loads = [
        pltpu.make_async_copy(wg_hbm.at[0], wg, wsem.at[0]),
        pltpu.make_async_copy(wu_hbm.at[0], wu, wsem.at[1]),
    ]
    for h in range(2):
        for f in range(NF):
            loads.append(
                pltpu.make_async_copy(
                    wd_hbm.at[0, :, pl.ds(h * half + f * fw, fw)], wd.at[h, f], wsem.at[2 + h * NF + f]
                )
            )
    for load in loads:
        load.start()

    eye = (iota((PAD, TOK), 0) == iota((PAD, TOK), 1)).astype(F32).astype(BF16)
    for f in range(NF):
        tok[0, f, 0] = mm(eye, tokens[:, f * fw:(f + 1) * fw]).astype(BF16)
    col = iota((TOK, COLS), 1)
    expert = sixth(col)
    slot = col - CAP * expert
    hit = jnp.zeros((TOK, COLS), F32)
    weight = jnp.zeros((TOK, COLS), F32)
    for k in range(TOP):
        named = routes[:, k:k + 1] == expert
        hit = jnp.where(named, 1.0, hit)
        weight = jnp.where(named, weights[:, k:k + 1], weight)
    lower = (iota((TOK, TOK), 0) > iota((TOK, TOK), 1)).astype(F32).astype(BF16)
    before = mm(lower, hit.astype(BF16))
    placed = jnp.where(before == slot.astype(F32), weight, 0.0)
    tm[0, 0] = mm(eye, placed.astype(BF16)).astype(BF16)

    pl.semaphore_wait(barrier, len(partners))

    copies = {}

    def send(name, src, dst, where):
        index = len(copies)
        copy = pltpu.make_async_remote_copy(
            src_ref=src, dst_ref=dst, send_sem=ssem.at[index], recv_sem=rsem.at[index],
            device_id=where, device_id_type=MESH,
        )
        copy.start()
        copies[name] = copy

    def arrive(name):
        copies[name].wait_recv()

    def near(p, f):
        for s, j in ((1, 1), (-1, 7), (2, 2), (-2, 6)):
            if f == 0:
                send(("m", p, j), tm.at[p, 0], tm.at[p, j], dev(dz=s))
        for s, j in ((1, 1), (-1, 7), (2, 2), (-2, 6)):
            send(("z", p, f, j), tok.at[p, f, 0], tok.at[p, f, j], dev(dz=s))

    def far(p, f):
        if f == 0:
            for j in (2, 6):
                arrive(("m", p, j))
            send(("m", p, 3), tm.at[p, 2], tm.at[p, 3], dev(dz=1))
            send(("m", p, 5), tm.at[p, 6], tm.at[p, 5], dev(dz=-1))
            send(("m", p, 4), tm.at[p, 2], tm.at[p, 4], dev(dz=2))
        for j in (2, 6):
            arrive(("z", p, f, j))
        send(("z", p, f, 3), tok.at[p, f, 2], tok.at[p, f, 3], dev(dz=1))
        send(("z", p, f, 5), tok.at[p, f, 6], tok.at[p, f, 5], dev(dz=-1))
        if f % 2 == 0:
            send(("z", p, f, 4), tok.at[p, f, 2], tok.at[p, f, 4], dev(dz=2))
        else:
            send(("z", p, f, 4), tok.at[p, f, 6], tok.at[p, f, 4], dev(dz=-2))

    def matrices(p):
        for j in (1, 7, 3, 4, 5):
            arrive(("m", p, j))
        table = tm[p].reshape(NZ * PAD, COLS)
        n = iota((PLANE, COLS), 0)
        q = sixth(n)
        want = (z * NY + ((y + (q >> 3)) & 3)) * CAP + (n - CAP * q)
        chosen = (iota((PLANE, COLS), 1) == want).astype(F32).astype(BF16)
        wide = mm(chosen, table, ((1,), (1,)))
        n = iota((PLANE, NZ * PAD), 0)
        keep = (sixth(n) & 7) == (iota((PLANE, NZ * PAD), 1) >> 4)
        pick[p] = jnp.where(keep & (wide != 0.0), 1.0, 0.0).astype(BF16)
        tall = mm(table, chosen, ((1,), (1,)))
        n = iota((NZ * PAD, PLANE), 1)
        keep = (sixth(n) & 7) == (iota((NZ * PAD, PLANE), 0) >> 4)
        mix[p] = jnp.where(keep, tall, 0.0).astype(BF16)

    def base(p):
        return 0 if p == 0 else 3 * PLANE

    def choose(p, f):
        if f == 0:
            matrices(p)
        for j in (1, 7, 3, 4, 5):
            arrive(("z", p, f, j))
        got = mm(pick[p], tok[p, f].reshape(NZ * PAD, fw)).astype(BF16)
        rows[c, f, base(p):base(p) + ROWS] = got[:ROWS]
        for d in (1, 2, 3):
            ysend[p, f, d - 1] = got[d * ROWS:(d + 1) * ROWS]
            send(
                ("y", p, f, d), ysend.at[p, f, d - 1],
                rows.at[c, f, pl.ds(base(p) + d * ROWS, ROWS)], dev(dy=d),
            )

    def to_sibling(name, f, start, size):
        block = rows.at[c, f, pl.ds(start, size)]
        send(("s", name, f), block, block, dev(dc=1))

    def onward(p, f):
        for d in (1, 2, 3):
            arrive(("y", p, f, d))
        if p == 0:
            block = rows.at[c, f, pl.ds(0, PLANE)]
            send(("x", 1, f), block, rows.at[c, f, pl.ds(PLANE, PLANE)], dev(dx=1))
            send(("x", -1, f), block, rows.at[c, f, pl.ds(2 * PLANE, PLANE)], dev(dx=-1))
        to_sibling(p, f, base(p), PLANE)

    def neighbours(f):
        arrive(("x", 1, f))
        arrive(("x", -1, f))
        to_sibling("x", f, PLANE, 2 * PLANE)

    def gate_up(f, h):
        depth = pl.ds(pl.multiple_of(h * half + f * fw, 128), fw)
        for q in range(2):
            block = rows[h, f, 2 * q * PLANE:2 * (q + 1) * PLANE]
            mine = pl.ds(2 * q * PLANE, 2 * PLANE)
            acc[mine, :HID] += mm(block, wg[depth, :])
            acc[mine, HID:] += mm(block, wu[depth, :])

    for f in range(NF):
        if f == 0:
            send(("m", 1, 0), tm.at[0, 0], tm.at[1, 0], dev(dx=2))
            near(0, 0)
        send(("o", f), tok.at[0, f, 0], tok.at[1, f, 0], dev(dx=2))
    acc[...] = jnp.zeros_like(acc)
    items = [(p, f) for p in range(2) for f in range(NF)]
    near(*items[1])
    for step in range(len(items) + 2):
        if step < len(items):
            far(*items[step])
        if step + 2 < len(items):
            p, f = items[step + 2]
            if p == 1:
                if f == 0:
                    arrive(("m", 1, 0))
                arrive(("o", f))
            near(p, f)
        if 1 <= step <= len(items):
            choose(*items[step - 1])
        if step >= 2:
            p, f = items[step - 2]
            onward(p, f)
            if p == 1:
                neighbours(f)
                if f == 0:
                    loads[0].wait()
                    loads[1].wait()
                gate_up(f, c)
                if f > 0:
                    for name in (0, 1, "x"):
                        arrive(("s", name, f - 1))
                    gate_up(f - 1, other)
    for name in (0, 1, "x"):
        arrive(("s", name, NF - 1))
    gate_up(NF - 1, other)
    for q in range(4):
        mine = pl.ds(q * PLANE, PLANE)
        gate = acc[mine, :HID]
        hid[mine] = (gate / (1.0 + jnp.exp(-gate)) * acc[mine, HID:]).astype(BF16)

    for load in loads[2:]:
        load.wait()
    for f in range(NF):
        for name in (("x", 1, f), ("x", -1, f), ("s", 0, f), ("s", 1, f), ("s", "x", f)):
            copies[name].wait_send()

    def down(f, h, dst):
        def body(q, carry):
            mine = pl.ds(pl.multiple_of(q * PLANE, PLANE), PLANE)
            dst[mine] = mm(hid[mine], wd[h, f]).astype(BF16)
            return carry
        lax.fori_loop(0, 4, body, 0)

    def down_other(f):
        down(f, other, rows.at[0, f])
        send(("d", f), rows.at[0, f], sib.at[f], dev(dc=1))

    def leave(f):
        arrive(("d", f))
        for q in (1, 2, 3, 0):
            mine = pl.ds(q * PLANE, PLANE)
            part[f, mine] = (part[f, mine].astype(F32) + sib[f, mine].astype(F32)).astype(BF16)
            if q == 1:
                send(("xb", -1, f), part.at[f, mine], xback.at[f, 1], dev(dx=-1))
            if q == 2:
                send(("xb", 1, f), part.at[f, mine], xback.at[f, 0], dev(dx=1))
            if q == 3:
                back(1, f)

    def back(p, f):
        for d in (1, 2, 3):
            send(
                ("yb", p, f, d), part.at[f, pl.ds(base(p) + d * ROWS, ROWS)],
                yback.at[p, f, pl.ds((d - 1) * ROWS, ROWS)], dev(dy=-d),
            )

    def home(f):
        arrive(("xb", -1, f))
        arrive(("xb", 1, f))
        mine = pl.ds(0, PLANE)
        total = part[f, mine].astype(F32) + xback[f, 0].astype(F32) + xback[f, 1].astype(F32)
        part[f, mine] = total.astype(BF16)
        back(0, f)

    def combine(p, f):
        for d in (1, 2, 3):
            arrive(("yb", p, f, d))
        total = mm(mix[p, :, :ROWS], part[f, base(p):base(p) + ROWS])
        total += mm(mix[p, :, ROWS:], yback[p, f])
        zpart[p, f] = total.astype(BF16).reshape(NZ, PAD, fw)
        send(("zf", p, f, 3), zpart.at[p, f, 3], zfar.at[p, f, 0], dev(dz=-1))
        send(("zf", p, f, 5), zpart.at[p, f, 5], zfar.at[p, f, 1], dev(dz=1))
        send(("zf", p, f, 4), zpart.at[p, f, 4], zfar.at[p, f, 2], dev(dz=-2 if f % 2 == 0 else 2))

    def closer(p, f):
        send(("zn", p, f, 1), zpart.at[p, f, 1], znear.at[p, f, 0], dev(dz=-1))
        send(("zn", p, f, 7), zpart.at[p, f, 7], znear.at[p, f, 1], dev(dz=1))
        for j in (3, 5, 4):
            arrive(("zf", p, f, j))
        two = zpart[p, f, 2].astype(F32) + zfar[p, f, 0].astype(F32)
        six = zpart[p, f, 6].astype(F32) + zfar[p, f, 1].astype(F32)
        if f % 2 == 0:
            two += zfar[p, f, 2].astype(F32)
        else:
            six += zfar[p, f, 2].astype(F32)
        zpart[p, f, 2] = two.astype(BF16)
        zpart[p, f, 6] = six.astype(BF16)
        send(("zn", p, f, 2), zpart.at[p, f, 2], znear.at[p, f, 2], dev(dz=-2))
        send(("zn", p, f, 6), zpart.at[p, f, 6], znear.at[p, f, 3], dev(dz=2))

    def gathered(p, f):
        for j in (1, 7, 2, 6):
            arrive(("zn", p, f, j))
        total = zpart[p, f, 0].astype(F32)
        for i in range(4):
            total += znear[p, f, i].astype(F32)
        return total

    def opposite(f):
        opp[0, f] = gathered(1, f).astype(BF16)
        send(("ob", f), opp.at[0, f], opp.at[1, f], dev(dx=2))

    def finish(f):
        total = gathered(0, f)
        arrive(("ob", f))
        total += opp[1, f].astype(F32)
        out[:, f * fw:(f + 1) * fw] = total.astype(BF16)

    down_other(0)
    down(0, c, part.at[0])
    for f in range(NF):
        if f + 1 < NF:
            down_other(f + 1)
        leave(f)
        if f + 1 < NF:
            down(f + 1, c, part.at[f + 1])
    for f in range(NF):
        combine(1, f)
        if f > 0:
            closer(0, f - 1)
        home(f)
        closer(1, f)
        if f > 0:
            finish(f - 1)
        combine(0, f)
        opposite(f)
    closer(0, NF - 1)
    finish(NF - 1)
    for name, copy in copies.items():
        if name[0] not in ("x", "s"):
            copy.wait_send()


COPIES = 1 + NF + 2 * 7 + 2 * NF * 7 + 2 * NF * 3 + 2 * NF + 3 * NF + NF + 2 * NF + 2 * NF * 3 + 2 * NF * 7 + NF


def per_device(tokens, routes, route_weights, w_gate, w_up, w_down):
    half = tokens.shape[1]
    fw = half // NF
    vmem = pl.BlockSpec(memory_space=pltpu.VMEM)
    hbm = pl.BlockSpec(memory_space=pl.ANY)
    result = pl.pallas_call(
        kernel,
        out_shape=jax.ShapeDtypeStruct((PAD, half), BF16),
        in_specs=[vmem, vmem, vmem, hbm, hbm, hbm],
        out_specs=vmem,
        scratch_shapes=[
            pltpu.VMEM((2, NF, NZ, PAD, fw), BF16),
            pltpu.VMEM((2, NZ, PAD, COLS), BF16),
            pltpu.VMEM((2, PLANE, NZ * PAD), BF16),
            pltpu.VMEM((2, NZ * PAD, PLANE), BF16),
            pltpu.VMEM((2, NF, 3, ROWS, fw), BF16),
            pltpu.VMEM((2, NF, 4 * PLANE, fw), BF16),
            pltpu.VMEM((2 * half, HID), BF16),
            pltpu.VMEM((2 * half, HID), BF16),
            pltpu.VMEM((2, NF, HID, fw), BF16),
            pltpu.VMEM((4 * PLANE, 2 * HID), F32),
            pltpu.VMEM((4 * PLANE, HID), BF16),
            pltpu.VMEM((NF, 4 * PLANE, fw), BF16),
            pltpu.VMEM((NF, 4 * PLANE, fw), BF16),
            pltpu.VMEM((NF, 2, PLANE, fw), BF16),
            pltpu.VMEM((2, NF, 3 * ROWS, fw), BF16),
            pltpu.VMEM((2, NF, NZ, PAD, fw), BF16),
            pltpu.VMEM((2, NF, 3, PAD, fw), BF16),
            pltpu.VMEM((2, NF, 4, PAD, fw), BF16),
            pltpu.VMEM((2, NF, PAD, fw), BF16),
            pltpu.SemaphoreType.DMA((2 + 2 * NF,)),
            pltpu.SemaphoreType.DMA((COPIES,)),
            pltpu.SemaphoreType.DMA((COPIES,)),
        ],
        compiler_params=pltpu.CompilerParams(
            collective_id=0, has_side_effects=True, vmem_limit_bytes=60 * 1024 * 1024
        ),
        name="experts",
    )(tokens, routes, route_weights, w_gate, w_up, w_down)
    return result[:TOK]


def solution(mesh):
    placed = (
        P(("attn", "exp"), "rep"),
        P(("attn", "exp"), None),
        P(("attn", "exp"), None),
        P("exp", None, ("attn", "rep")),
        P("exp", None, ("attn", "rep")),
        P("exp", ("attn", "rep"), None),
    )
    return jax.shard_map(
        per_device, mesh=mesh, in_specs=placed, out_specs=P(("attn", "exp"), "rep"), check_vma=False
    )
```

```python
import functools

import jax
import jax.numpy as jnp
from jax import lax
from jax.experimental import pallas as pl
from jax.experimental.pallas import tpu as pltpu
from jax.sharding import PartitionSpec as P

MESH = pl.DeviceIdType.MESH
NX, NZ, NY = 4, 8, 4
WIDTHS = (512, 768, 768, 768, 512, 256)
NF = len(WIDTHS)
STARTS = tuple(sum(WIDTHS[:f]) for f in range(NF))
TOK, PAD, TOP, CAP, HID = 12, 16, 8, 6, 256
COLS = 256
ROWS = NZ * CAP
PLANE = NY * ROWS
F32, BF16 = jnp.float32, jnp.bfloat16


def mm(a, b, dims=((1,), (0,))):
    return lax.dot_general(a, b, (dims, ((), ())), preferred_element_type=F32)


def iota(shape, dim):
    return lax.broadcasted_iota(jnp.int32, shape, dim)


def sixth(n):
    return (n * 10923) >> 16


def kernel(
    tokens_hbm, routes_hbm, weights_hbm, wg_hbm, wu_hbm, wd_hbm, out_hbm,
    tokens, routes, weights, out, tok, tm, pick, mix, ysend, rows, wg, wu, wd, acc, hid,
    part, sib, xback, yback, zpart, zfar, znear, opp,
    isem, osem, wsem, ssem, rsem,
):
    half = tokens.shape[1]
    x = lax.axis_index("attn")
    e = lax.axis_index("exp")
    c = lax.axis_index("rep")
    z, y = e // NY, lax.rem(e, NY)
    other = 1 - c

    def dev(dx=0, dz=0, dy=0, dc=0):
        return (
            lax.rem(x + dx + NX, NX),
            lax.rem(z + dz + NZ, NZ) * NY + lax.rem(y + dy + NY, NY),
            lax.rem(c + dc, 2),
        )

    partners = [dev(dx=1), dev(dx=-1), dev(dx=2), dev(dc=1)]
    partners += [dev(dy=d) for d in (1, 2, 3)]
    partners += [dev(dz=d) for d in (1, -1, 2, -2)]
    barrier = pltpu.get_barrier_semaphore()
    for partner in partners:
        pl.semaphore_signal(barrier, inc=1, device_id=partner, device_id_type=MESH)

    inputs = [
        pltpu.make_async_copy(src, dst, isem.at[i])
        for i, (src, dst) in enumerate(((tokens_hbm, tokens), (routes_hbm, routes), (weights_hbm, weights)))
    ]
    for copy in inputs:
        copy.start()
    loads = [
        pltpu.make_async_copy(wg_hbm.at[0], wg, wsem.at[0]),
        pltpu.make_async_copy(wu_hbm.at[0], wu, wsem.at[1]),
    ]
    for h in range(2):
        for f in range(NF):
            loads.append(
                pltpu.make_async_copy(
                    wd_hbm.at[0, :, pl.ds(h * half + STARTS[f], WIDTHS[f])], wd[f].at[h], wsem.at[2 + h * NF + f]
                )
            )
    for load in loads:
        load.start()
    for copy in inputs:
        copy.wait()

    eye = (iota((PAD, TOK), 0) == iota((PAD, TOK), 1)).astype(F32).astype(BF16)
    for f in range(NF):
        tok[f][0, 0] = mm(eye, tokens[:, STARTS[f]:STARTS[f] + WIDTHS[f]]).astype(BF16)
    col = iota((TOK, COLS), 1)
    expert = sixth(col)
    slot = col - CAP * expert
    square = (iota((TOK, TOK), 0) == iota((TOK, TOK), 1)).astype(F32).astype(BF16)
    names = mm(square, routes[...].astype(F32).astype(BF16), ((1,), (1,))).astype(jnp.int32)
    gains = mm(square, weights[...].astype(BF16), ((1,), (1,)))
    hit = jnp.zeros((TOK, COLS), F32)
    weight = jnp.zeros((TOK, COLS), F32)
    for k in range(TOP):
        named = names[:, k:k + 1] == expert
        hit = jnp.where(named, 1.0, hit)
        weight = jnp.where(named, gains[:, k:k + 1], weight)
    lower = (iota((TOK, TOK), 0) > iota((TOK, TOK), 1)).astype(F32).astype(BF16)
    before = mm(lower, hit.astype(BF16))
    placed = jnp.where(before == slot.astype(F32), weight, 0.0)
    tm[0, 0] = mm(eye, placed.astype(BF16)).astype(BF16)

    pl.semaphore_wait(barrier, len(partners))

    inward, outward, whole = {}, {}, {}
    free = list(range(ssem.shape[0]))
    results = []

    def send(out_key, in_key, src, dst, where, block):
        if in_key not in inward:
            inward[in_key] = len(inward)
        if out_key not in outward:
            outward[out_key] = free.pop(0)
            whole[out_key] = block
        pltpu.make_async_remote_copy(
            src_ref=src, dst_ref=dst, send_sem=ssem.at[outward[out_key]], recv_sem=rsem.at[inward[in_key]],
            device_id=where, device_id_type=MESH,
        ).start()

    def waiter(block, sends, arrivals):
        return pltpu.make_async_remote_copy(
            src_ref=block, dst_ref=block, send_sem=ssem.at[sends], recv_sem=rsem.at[arrivals],
            device_id=partners[3], device_id_type=MESH,
        )

    def arrive(key, block):
        waiter(block, 0, inward[key]).wait_recv()

    def sent(keys):
        for key in keys:
            slot = outward.pop(key)
            waiter(whole[key], slot, 0).wait_send()
            free.append(slot)

    hops = ((1, 1, "b"), (-1, 7, "b"), (2, 2, "a"), (-2, 6, "a"))

    def near(p, f):
        if f == 0:
            for s, j, part_of in hops:
                send(("m", p), ("m" + part_of, p), tm.at[p, 0], tm.at[p, j], dev(dz=s), tm.at[p, pl.ds(0, 4)])
        for s, j, part_of in hops:
            send(
                ("z", p, f), ("z" + part_of, p, f), tok[f].at[p, 0], tok[f].at[p, j], dev(dz=s),
                tok[f].at[p, pl.ds(0, 4)],
            )

    def far(p, f):
        if f == 0:
            arrive(("ma", p), tm.at[p, pl.ds(0, 2)])
            for s, i, j in ((1, 2, 3), (-1, 6, 5), (2, 2, 4)):
                send(("mf", p), ("mb", p), tm.at[p, i], tm.at[p, j], dev(dz=s), tm.at[p, pl.ds(0, 3)])
        arrive(("za", p, f), tok[f].at[p, pl.ds(0, 2)])
        for s, i, j in ((1, 2, 3), (-1, 6, 5), (2, 2, 4) if f % 2 == 0 else (-2, 6, 4)):
            send(
                ("zf", p, f), ("zb", p, f), tok[f].at[p, i], tok[f].at[p, j], dev(dz=s),
                tok[f].at[p, pl.ds(0, 3)],
            )

    def matrices(p):
        arrive(("mb", p), tm.at[p, pl.ds(0, 5)])
        table = tm[p].reshape(NZ * PAD, COLS)
        n = iota((PLANE, COLS), 0)
        q = sixth(n)
        want = (z * NY + ((y + (q >> 3)) & 3)) * CAP + (n - CAP * q)
        chosen = (iota((PLANE, COLS), 1) == want).astype(F32).astype(BF16)
        wide = mm(chosen, table, ((1,), (1,)))
        n = iota((PLANE, NZ * PAD), 0)
        keep = (sixth(n) & 7) == (iota((PLANE, NZ * PAD), 1) >> 4)
        pick[p] = jnp.where(keep & (wide != 0.0), 1.0, 0.0).astype(BF16)
        tall = mm(table, chosen, ((1,), (1,)))
        n = iota((NZ * PAD, PLANE), 1)
        keep = (sixth(n) & 7) == (iota((NZ * PAD, PLANE), 0) >> 4)
        mix[p] = jnp.where(keep, tall, 0.0).astype(BF16)

    def base(p):
        return 0 if p == 0 else 3 * PLANE

    def choose(p, f):
        if f == 0:
            matrices(p)
        arrive(("zb", p, f), tok[f].at[p, pl.ds(0, 5)])
        got = mm(pick[p], tok[f][p].reshape(NZ * PAD, WIDTHS[f])).astype(BF16)
        rows[f][c, base(p):base(p) + ROWS] = got[:ROWS]
        for d in (1, 2, 3):
            ysend[f][p, d - 1] = got[d * ROWS:(d + 1) * ROWS]
            send(
                ("y", p, f), ("y", p, f), ysend[f].at[p, d - 1],
                rows[f].at[c, pl.ds(base(p) + d * ROWS, ROWS)], dev(dy=d), ysend[f].at[p],
            )

    def to_sibling(f, start, size):
        block = rows[f].at[c, pl.ds(start, size)]
        send(("s", f), ("s", f), block, block, dev(dc=1), rows[f].at[c])

    def from_sibling(f):
        arrive(("s", f), rows[f].at[other])

    def onward(p, f):
        arrive(("y", p, f), rows[f].at[c, pl.ds(base(p) + ROWS, 3 * ROWS)])
        if p == 0:
            block = rows[f].at[c, pl.ds(0, PLANE)]
            both_ways = rows[f].at[c, pl.ds(PLANE, 2 * PLANE)]
            send(("x", f), ("x", f), block, rows[f].at[c, pl.ds(PLANE, PLANE)], dev(dx=1), both_ways)
            send(("x", f), ("x", f), block, rows[f].at[c, pl.ds(2 * PLANE, PLANE)], dev(dx=-1), both_ways)
        to_sibling(f, base(p), PLANE)

    def neighbours(f):
        arrive(("x", f), rows[f].at[c, pl.ds(PLANE, 2 * PLANE)])
        to_sibling(f, PLANE, 2 * PLANE)

    def gate_up(f, h):
        depth = pl.ds(pl.multiple_of(h * half + STARTS[f], 128), WIDTHS[f])
        for q in range(2):
            block = rows[f][h, 2 * q * PLANE:2 * (q + 1) * PLANE]
            mine = pl.ds(2 * q * PLANE, 2 * PLANE)
            acc[mine, :HID] += mm(block, wg[depth, :])
            acc[mine, HID:] += mm(block, wu[depth, :])

    items = [(p, f) for p in range(2) for f in range(NF)]
    near(*items[0])
    send(("o", 0), ("om", 0), tm.at[0, 0], tm.at[1, 0], dev(dx=2), tm.at[0, 0])
    for f in range(NF):
        send(("oz", f), ("oz", f), tok[f].at[0, 0], tok[f].at[1, 0], dev(dx=2), tok[f].at[0, 0])
    acc[...] = jnp.zeros_like(acc)
    near(*items[1])

    def further(step):
        if step < len(items):
            far(*items[step])
        for later in (2, 3) if step == 0 else (step + 3,):
            if later < len(items):
                p, f = items[later]
                if p == 1:
                    if f == 0:
                        arrive(("om", 0), tm.at[0, 0])
                    arrive(("oz", f), tok[f].at[0, 0])
                near(p, f)

    further(0)
    further(1)
    for step in range(len(items) + 2):
        if step < len(items):
            further(step + 2)
            choose(*items[step])
        if step >= 2:
            p, f = items[step - 2]
            if p == 1 and f > 0:
                from_sibling(f - 1)
                gate_up(f - 1, other)
            onward(p, f)
            if p == 1:
                neighbours(f)
                if f == 0:
                    loads[0].wait()
                    loads[1].wait()
                gate_up(f, c)
    sent([key for key in outward if key != ("s", NF - 1)])
    from_sibling(NF - 1)
    gate_up(NF - 1, other)
    for q in range(4):
        mine = pl.ds(q * PLANE, PLANE)
        gate = acc[mine, :HID]
        hid[mine] = (gate / (1.0 + jnp.exp(-gate)) * acc[mine, HID:]).astype(BF16)

    for load in loads[2:]:
        load.wait()
    sent(list(outward))

    inner, outer = pl.ds(PLANE, 2 * PLANE), pl.ds(3 * PLANE, PLANE)
    first = pl.ds(0, PLANE)

    def down(f, h, dst, parts):
        for mine in parts:
            dst[mine] = mm(hid[mine], wd[f][h]).astype(BF16)

    def down_both(f):
        scratch = rows[f].at[0]
        down(f, other, scratch, (inner,))
        send(("d", f), ("da", f), scratch.at[inner], sib[f].at[inner], dev(dc=1), scratch)
        down(f, c, part[f], (inner,))
        down(f, other, scratch, (outer, first))
        send(("d", f), ("db", f), scratch.at[outer], sib[f].at[outer], dev(dc=1), scratch)
        send(("d", f), ("db", f), scratch.at[first], sib[f].at[first], dev(dc=1), scratch)
        down(f, c, part[f], (outer, first))

    def both(f, mine):
        part[f][mine] = (part[f][mine].astype(F32) + sib[f][mine].astype(F32)).astype(BF16)

    def leave(f):
        arrive(("da", f), sib[f].at[inner])
        both(f, inner)
        for d, q, place in ((-1, 1, 1), (1, 2, 0)):
            send(
                ("xb", f), ("xb", f), part[f].at[pl.ds(q * PLANE, PLANE)], xback[f].at[place], dev(dx=d), xback[f]
            )

    def leave_opposite(f):
        arrive(("db", f), sib[f].at[inner])
        both(f, outer)
        both(f, first)

    def back(p, f):
        for d in (1, 2, 3):
            send(
                ("yb", p, f), ("yb", p, f), part[f].at[pl.ds(base(p) + d * ROWS, ROWS)],
                yback[f].at[p, pl.ds((d - 1) * ROWS, ROWS)], dev(dy=-d), yback[f].at[p],
            )

    def home(f):
        arrive(("xb", f), xback[f])
        total = part[f][first].astype(F32) + xback[f][0].astype(F32) + xback[f][1].astype(F32)
        part[f][first] = total.astype(BF16)
        back(0, f)

    def combine(p, f):
        arrive(("yb", p, f), yback[f].at[p])
        total = mm(mix[p, :, :ROWS], part[f][base(p):base(p) + ROWS])
        total += mm(mix[p, :, ROWS:], yback[f][p])
        zpart[f][p] = total.astype(BF16).reshape(NZ, PAD, WIDTHS[f])
        for s, j, place in ((-1, 3, 0), (1, 5, 1), (-2 if f % 2 == 0 else 2, 4, 2)):
            send(("zi", p, f), ("zi", p, f), zpart[f].at[p, j], zfar[f].at[p, place], dev(dz=s), zfar[f].at[p])

    def closer(p, f):
        def home_by(s, j, place):
            send(("zn", p, f), ("zn", p, f), zpart[f].at[p, j], znear[f].at[p, place], dev(dz=s), znear[f].at[p])

        home_by(-1, 1, 0)
        home_by(1, 7, 1)
        arrive(("zi", p, f), zfar[f].at[p])
        two = zpart[f][p, 2].astype(F32) + zfar[f][p, 0].astype(F32)
        six = zpart[f][p, 6].astype(F32) + zfar[f][p, 1].astype(F32)
        if f % 2 == 0:
            two += zfar[f][p, 2].astype(F32)
        else:
            six += zfar[f][p, 2].astype(F32)
        zpart[f][p, 2] = two.astype(BF16)
        zpart[f][p, 6] = six.astype(BF16)
        home_by(-2, 2, 2)
        home_by(2, 6, 3)

    def gathered(p, f):
        arrive(("zn", p, f), znear[f].at[p])
        total = zpart[f][p, 0].astype(F32)
        for i in range(4):
            total += znear[f][p, i].astype(F32)
        return total

    def opposite(f):
        opp[f][0] = gathered(1, f).astype(BF16)
        send(("ob", f), ("ob", f), opp[f].at[0], opp[f].at[1], dev(dx=2), opp[f].at[0])

    def finish(f):
        total = gathered(0, f)
        arrive(("ob", f), opp[f].at[0])
        total += opp[f][1].astype(F32)
        mine = pl.ds(STARTS[f], WIDTHS[f])
        out[:, mine] = total.astype(BF16)
        results.append(pltpu.make_async_copy(out.at[:, mine], out_hbm.at[:, mine], osem.at[f]))
        results[-1].start()

    down_both(0)
    down_both(1)
    leave(0)
    down_both(2)
    leave_opposite(0)
    leave(1)
    back(1, 0)
    down_both(3)
    leave_opposite(1)
    leave(2)
    leave_opposite(2)
    back(1, 1)
    leave(3)
    back(1, 2)
    down_both(4)
    leave_opposite(3)
    down_both(5)
    back(1, 3)
    home(0)
    leave(4)
    leave_opposite(4)
    leave(5)
    back(1, 4)
    combine(1, 0)
    leave_opposite(5)
    back(1, 5)
    combine(1, 1)
    closer(1, 0)
    home(1)
    combine(1, 2)
    closer(1, 1)
    opposite(0)
    combine(1, 3)
    closer(1, 2)
    home(2)
    combine(0, 0)
    opposite(1)
    closer(1, 3)
    combine(1, 4)
    combine(1, 5)
    opposite(2)
    closer(0, 0)
    home(3)
    combine(0, 1)
    opposite(3)
    closer(1, 4)
    closer(1, 5)
    combine(0, 2)
    home(4)
    closer(0, 1)
    opposite(4)
    home(5)
    opposite(5)
    combine(0, 3)
    finish(0)
    closer(0, 2)
    combine(0, 4)
    finish(1)
    combine(0, 5)
    closer(0, 3)
    finish(2)
    closer(0, 4)
    closer(0, 5)
    finish(3)
    finish(4)
    finish(5)
    sent(list(outward))
    for copy in results:
        copy.wait()


def per_device(tokens, routes, route_weights, w_gate, w_up, w_down):
    half = tokens.shape[1]
    hbm = pl.BlockSpec(memory_space=pl.ANY)

    def chunked(*lead):
        return [pltpu.VMEM((*lead, width), BF16) for width in WIDTHS]

    result = pl.pallas_call(
        kernel,
        out_shape=jax.ShapeDtypeStruct((PAD, half), BF16),
        in_specs=[hbm] * 6,
        out_specs=hbm,
        scratch_shapes=[
            pltpu.VMEM((TOK, half), BF16),
            pltpu.VMEM((TOP, TOK), jnp.int32),
            pltpu.VMEM((TOP, TOK), F32),
            pltpu.VMEM((PAD, half), BF16),
            chunked(2, NZ, PAD),
            pltpu.VMEM((2, NZ, PAD, COLS), BF16),
            pltpu.VMEM((2, PLANE, NZ * PAD), BF16),
            pltpu.VMEM((2, NZ * PAD, PLANE), BF16),
            chunked(2, 3, ROWS),
            chunked(2, 4 * PLANE),
            pltpu.VMEM((2 * half, HID), BF16),
            pltpu.VMEM((2 * half, HID), BF16),
            chunked(2, HID),
            pltpu.VMEM((4 * PLANE, 2 * HID), F32),
            pltpu.VMEM((4 * PLANE, HID), BF16),
            chunked(4 * PLANE),
            chunked(4 * PLANE),
            chunked(2, PLANE),
            chunked(2, 3 * ROWS),
            chunked(2, NZ, PAD),
            chunked(2, 3, PAD),
            chunked(2, 4, PAD),
            chunked(2, PAD),
            pltpu.SemaphoreType.DMA((3,)),
            pltpu.SemaphoreType.DMA((NF,)),
            pltpu.SemaphoreType.DMA((2 + 2 * NF,)),
            pltpu.SemaphoreType.DMA((5 + 9 * NF,)),
            pltpu.SemaphoreType.DMA((5 + 19 * NF,)),
        ],
        compiler_params=pltpu.CompilerParams(
            collective_id=0, has_side_effects=True, vmem_limit_bytes=60 * 1024 * 1024
        ),
        name="experts",
    )(tokens, routes.T, route_weights.T, w_gate, w_up, w_down)
    return result[:TOK]


def solution(mesh):
    placed = (
        P(("attn", "exp"), "rep"),
        P(("attn", "exp"), None),
        P(("attn", "exp"), None),
        P("exp", None, ("attn", "rep")),
        P("exp", None, ("attn", "rep")),
        P("exp", ("attn", "rep"), None),
    )
    return jax.shard_map(
        per_device, mesh=mesh, in_specs=placed, out_specs=P(("attn", "exp"), "rep"), check_vma=False
    )
```

```python
import functools

import jax
import jax.numpy as jnp
from jax import lax
from jax.experimental import pallas as pl
from jax.experimental.pallas import tpu as pltpu
from jax.sharding import PartitionSpec as P

MESH = pl.DeviceIdType.MESH
NX, NZ, NY = 4, 8, 4
WIDTHS = (512, 768, 768, 768, 512, 256)
NF = len(WIDTHS)
STARTS = tuple(sum(WIDTHS[:f]) for f in range(NF))
TOK, PAD, TOP, CAP, HID = 12, 16, 8, 6, 256
COLS = 256
ROWS = NZ * CAP
PLANE = NY * ROWS
F32, BF16 = jnp.float32, jnp.bfloat16


def mm(a, b, dims=((1,), (0,))):
    return lax.dot_general(a, b, (dims, ((), ())), preferred_element_type=F32)


def iota(shape, dim):
    return lax.broadcasted_iota(jnp.int32, shape, dim)


def sixth(n):
    return (n * 10923) >> 16


def kernel(
    tokens_hbm, routes_hbm, weights_hbm, wg_hbm, wu_hbm, wd_hbm, out_hbm,
    tokens, routes, weights, out, tok, tm, pick, mix, ysend, rows, wg, wu, wd, acc, hid,
    part, xback, yback, zpart, zfar, znear, zlast, opp,
    isem, osem, wsem, ssem, rsem,
):
    half = tokens.shape[1]
    x = lax.axis_index("attn")
    e = lax.axis_index("exp")
    c = lax.axis_index("rep")
    z, y = e // NY, lax.rem(e, NY)
    other = 1 - c

    def dev(dx=0, dz=0, dy=0, dc=0):
        return (
            lax.rem(x + dx + NX, NX),
            lax.rem(z + dz + NZ, NZ) * NY + lax.rem(y + dy + NY, NY),
            lax.rem(c + dc, 2),
        )

    partners = [dev(dx=1), dev(dx=-1), dev(dx=2), dev(dc=1)]
    partners += [dev(dy=d) for d in (1, 2, 3)]
    partners += [dev(dz=d) for d in (1, -1, 2, -2, 3, -3, 4)]
    barrier = pltpu.get_barrier_semaphore()
    for partner in partners:
        pl.semaphore_signal(barrier, inc=1, device_id=partner, device_id_type=MESH)

    inputs = [
        pltpu.make_async_copy(src, dst, isem.at[i])
        for i, (src, dst) in enumerate(((tokens_hbm, tokens), (routes_hbm, routes), (weights_hbm, weights)))
    ]
    for copy in inputs:
        copy.start()
    loads = [
        pltpu.make_async_copy(wg_hbm.at[0], wg, wsem.at[0]),
        pltpu.make_async_copy(wu_hbm.at[0], wu, wsem.at[1]),
    ]
    for f in range(NF):
        mine = pl.ds(pl.multiple_of(c * half + STARTS[f], 128), WIDTHS[f])
        loads.append(pltpu.make_async_copy(wd_hbm.at[0, :, mine], wd[f].at[pl.ds(0, HID)], wsem.at[2]))
    narrow = wg.at[pl.ds(0, half)]

    eye = (iota((PAD, TOK), 0) == iota((PAD, TOK), 1)).astype(F32).astype(BF16)

    def placement():
        col = iota((TOK, COLS), 1)
        expert = sixth(col)
        slot = col - CAP * expert
        square = (iota((TOK, TOK), 0) == iota((TOK, TOK), 1)).astype(F32).astype(BF16)
        names = mm(square, routes[...].astype(F32).astype(BF16), ((1,), (1,))).astype(jnp.int32)
        gains = mm(square, weights[...].astype(BF16), ((1,), (1,)))
        hit = jnp.zeros((TOK, COLS), F32)
        weight = jnp.zeros((TOK, COLS), F32)
        for k in range(TOP):
            named = names[:, k:k + 1] == expert
            hit = jnp.where(named, 1.0, hit)
            weight = jnp.where(named, gains[:, k:k + 1], weight)
        lower = (iota((TOK, TOK), 0) > iota((TOK, TOK), 1)).astype(F32).astype(BF16)
        before = mm(lower, hit.astype(BF16))
        placed = jnp.where(before == slot.astype(F32), weight, 0.0)
        tm[0, 0] = mm(eye, placed.astype(BF16)).astype(BF16)

    def padded(f):
        tok[f][0, 0] = mm(eye, tokens[:, STARTS[f]:STARTS[f] + WIDTHS[f]]).astype(BF16)

    inputs[1].wait()
    inputs[2].wait()
    placement()
    inputs[0].wait()
    padded(0)
    padded(1)

    pl.semaphore_wait(barrier, len(partners))

    inward, outward, whole = {}, {}, {}
    free = list(range(ssem.shape[0]))

    def send(out_key, in_key, src, dst, where, block):
        if in_key not in inward:
            inward[in_key] = len(inward)
        if out_key not in outward:
            outward[out_key] = free.pop(0)
            whole[out_key] = block
        pltpu.make_async_remote_copy(
            src_ref=src, dst_ref=dst, send_sem=ssem.at[outward[out_key]], recv_sem=rsem.at[inward[in_key]],
            device_id=where, device_id_type=MESH,
        ).start()

    def waiter(block, sends, arrivals):
        return pltpu.make_async_remote_copy(
            src_ref=block, dst_ref=block, send_sem=ssem.at[sends], recv_sem=rsem.at[arrivals],
            device_id=partners[3], device_id_type=MESH,
        )

    def arrive(key, block):
        waiter(block, 0, inward[key]).wait_recv()

    def sent(keys):
        for key in keys:
            slot = outward.pop(key)
            waiter(whole[key], slot, 0).wait_send()
            free.insert(0, slot)

    hops = ((1, 1, "b"), (-1, 7, "b"), (2, 2, "a"), (-2, 6, "a"))

    def near(p, f):
        if f == 0:
            for s, j, part_of in hops:
                send(("m", p), ("m" + part_of, p), tm.at[p, 0], tm.at[p, j], dev(dz=s), tm.at[p, pl.ds(0, 4)])
        for s, j, part_of in hops:
            send(
                ("z", p, f), ("z" + part_of, p, f), tok[f].at[p, 0], tok[f].at[p, j], dev(dz=s),
                tok[f].at[p, pl.ds(0, 4)],
            )

    def far(p, f):
        if f == 0:
            arrive(("ma", p), tm.at[p, pl.ds(0, 2)])
            for s, i, j in ((1, 2, 3), (-1, 6, 5), (2, 2, 4)):
                send(("mf", p), ("mb", p), tm.at[p, i], tm.at[p, j], dev(dz=s), tm.at[p, pl.ds(0, 3)])
        arrive(("za", p, f), tok[f].at[p, pl.ds(0, 2)])
        for s, i, j in ((1, 2, 3), (-1, 6, 5), (2, 2, 4) if f % 2 == 0 else (-2, 6, 4)):
            send(
                ("zf", p, f), ("zb", p, f), tok[f].at[p, i], tok[f].at[p, j], dev(dz=s),
                tok[f].at[p, pl.ds(0, 3)],
            )

    def matrices(p):
        arrive(("mb", p), tm.at[p, pl.ds(0, 5)])
        table = tm[p].reshape(NZ * PAD, COLS)
        n = iota((PLANE, COLS), 0)
        q = sixth(n)
        want = (z * NY + ((y + (q >> 3)) & 3)) * CAP + (n - CAP * q)
        chosen = (iota((PLANE, COLS), 1) == want).astype(F32).astype(BF16)
        wide = mm(chosen, table, ((1,), (1,)))
        n = iota((PLANE, NZ * PAD), 0)
        keep = (sixth(n) & 7) == (iota((PLANE, NZ * PAD), 1) >> 4)
        pick[p] = jnp.where(keep & (wide != 0.0), 1.0, 0.0).astype(BF16)
        tall = mm(table, chosen, ((1,), (1,)))
        n = iota((NZ * PAD, PLANE), 1)
        keep = (sixth(n) & 7) == (iota((NZ * PAD, PLANE), 0) >> 4)
        mix[p] = jnp.where(keep, tall, 0.0).astype(BF16)

    def base(p):
        return 0 if p == 0 else 3 * PLANE

    def sideways(f, start, size):
        for d, q in ((1, 1), (-1, 2)):
            send(
                ("x", f), ("x", f), rows[f].at[c, pl.ds(start, size)],
                rows[f].at[c, pl.ds(q * PLANE + start, size)], dev(dx=d), rows[f].at[c, pl.ds(PLANE, 2 * PLANE)],
            )

    def choose(p, f):
        if f == 0:
            matrices(p)
        arrive(("zb", p, f), tok[f].at[p, pl.ds(0, 5)])
        got = mm(pick[p], tok[f][p].reshape(NZ * PAD, WIDTHS[f])).astype(BF16)
        rows[f][c, base(p):base(p) + ROWS] = got[:ROWS]
        if p == 0:
            sideways(f, 0, ROWS)
        for d in (1, 2, 3):
            ysend[f][p, d - 1] = got[d * ROWS:(d + 1) * ROWS]
            send(
                ("y", p, f), ("y", p, f), ysend[f].at[p, d - 1],
                rows[f].at[c, pl.ds(base(p) + d * ROWS, ROWS)], dev(dy=d), ysend[f].at[p],
            )

    def to_sibling(f, start, size):
        block = rows[f].at[c, pl.ds(start, size)]
        send(("s", f), ("s", f), block, block, dev(dc=1), rows[f].at[c])

    def from_sibling(f):
        arrive(("s", f), rows[f].at[other])

    def onward(p, f):
        arrive(("y", p, f), rows[f].at[c, pl.ds(base(p) + ROWS, 3 * ROWS)])
        if p == 0:
            sideways(f, ROWS, PLANE - ROWS)
        to_sibling(f, base(p), PLANE)

    def neighbours(f):
        arrive(("x", f), rows[f].at[c, pl.ds(PLANE, 2 * PLANE)])
        to_sibling(f, PLANE, 2 * PLANE)

    def gate_up(f, h):
        depth = pl.ds(pl.multiple_of(h * half + STARTS[f], 128), WIDTHS[f])
        for q in range(2):
            block = rows[f][h, 2 * q * PLANE:2 * (q + 1) * PLANE]
            mine = pl.ds(2 * q * PLANE, 2 * PLANE)
            acc[mine, :HID] += mm(block, wg[depth, :])
            acc[mine, HID:] += mm(block, wu[depth, :])

    items = [(p, f) for p in range(2) for f in range(NF)]
    near(*items[0])
    send(("o", 0), ("om", 0), tm.at[0, 0], tm.at[1, 0], dev(dx=2), tm.at[0, 0])
    near(*items[1])
    for f in range(NF):
        if f > 1:
            padded(f)
        send(("oz",), ("oz",), tok[f].at[0, 0], tok[f].at[1, 0], dev(dx=2), out)
    for load in loads:
        load.start()
    for f in range(NF):
        theirs = pl.ds(pl.multiple_of(other * half + STARTS[f], 128), WIDTHS[f])
        send(("w",), ("w",), wd_hbm.at[0, :, theirs], wd[f].at[pl.ds(HID, HID)], dev(dc=1), narrow)
    acc[...] = jnp.zeros_like(acc)

    def further(step):
        if step < len(items):
            far(*items[step])
        for later in (2, 3) if step == 0 else (step + 3,):
            if later < len(items):
                p, f = items[later]
                if p == 1:
                    if f == 0:
                        arrive(("om", 0), tm.at[0, 0])
                        arrive(("oz",), out)
                near(p, f)

    further(0)
    further(1)
    for step in range(len(items) + 2):
        if step < len(items):
            if step > 0:
                further(step + 2)
            choose(*items[step])
            if step == 0:
                further(2)
        if step >= 2:
            p, f = items[step - 2]
            if p == 1:
                sent([("z", 0, f), ("zf", 0, f), ("y", 0, f)])
            if p == 1 and f > 0:
                from_sibling(f - 1)
                gate_up(f - 1, other)
            onward(p, f)
            if p == 1:
                neighbours(f)
                if f == 0:
                    loads[0].wait()
                    loads[1].wait()
                gate_up(f, c)
    sent([key for key in outward if key != ("s", NF - 1)])
    from_sibling(NF - 1)
    gate_up(NF - 1, other)
    inner, outer = pl.ds(PLANE, 2 * PLANE), pl.ds(3 * PLANE, PLANE)
    first = pl.ds(0, PLANE)
    ours, theirs = pl.ds(0, HID), pl.ds(HID, HID)
    for key, mine in (("inner", inner), ("edge", outer), ("edge", first)):
        gate = acc[mine, :HID]
        hid[mine, ours] = (gate / (1.0 + jnp.exp(-gate)) * acc[mine, HID:]).astype(BF16)
        send(("h",), ("h", key), hid.at[mine, ours], hid.at[mine, theirs], dev(dc=1), hid.at[:, ours])

    sent([key for key in outward if key != ("h",)])
    pltpu.make_async_copy(narrow, narrow, wsem.at[2]).wait()
    arrive(("w",), narrow)
    arrive(("h", "inner"), hid.at[inner, theirs])

    def down(f, mine):
        part[f][mine] = mm(hid[mine], wd[f][...]).astype(BF16)

    def leave(f):
        down(f, inner)
        for d, q, place in ((-1, 1, 1), (1, 2, 0)):
            send(
                ("xb", f), ("xb", f), part[f].at[pl.ds(q * PLANE, PLANE)], xback[f].at[place], dev(dx=d), xback[f]
            )

    def leave_opposite(f):
        if f == 0:
            arrive(("h", "edge"), hid.at[inner, theirs])
        down(f, outer)
        down(f, first)

    def back(p, f):
        for d in (1, 2, 3):
            send(
                ("yb", p, f), ("yb", p, f), part[f].at[pl.ds(base(p) + d * ROWS, ROWS)],
                yback[f].at[p, pl.ds((d - 1) * ROWS, ROWS)], dev(dy=-d), yback[f].at[p],
            )

    def home(f):
        arrive(("xb", f), xback[f])
        total = part[f][first].astype(F32) + xback[f][0].astype(F32) + xback[f][1].astype(F32)
        part[f][first] = total.astype(BF16)
        back(0, f)

    def combine(p, f):
        arrive(("yb", p, f), yback[f].at[p])
        total = mm(mix[p, :, :ROWS], part[f][base(p):base(p) + ROWS])
        total += mm(mix[p, :, ROWS:], yback[f][p])
        zpart[f][p] = total.astype(BF16).reshape(NZ, PAD, WIDTHS[f])
        if (p, f) == (0, NF - 1):
            for j in range(1, NZ):
                send(("zi", p, f), ("zi", p, f), zpart[f].at[p, j], zlast.at[j - 1], dev(dz=-j), zlast)
            return
        for s, j, place in ((-1, 3, 0), (1, 5, 1), (-2 if f % 2 == 0 else 2, 4, 2)):
            send(("zi", p, f), ("zi", p, f), zpart[f].at[p, j], zfar[f].at[p, place], dev(dz=s), zfar[f].at[p])

    def closer(p, f):
        def home_by(s, j, place):
            send(("zn", p, f), ("zn", p, f), zpart[f].at[p, j], znear[f].at[p, place], dev(dz=s), znear[f].at[p])

        home_by(-1, 1, 0)
        home_by(1, 7, 1)
        arrive(("zi", p, f), zfar[f].at[p])
        two = zpart[f][p, 2].astype(F32) + zfar[f][p, 0].astype(F32)
        six = zpart[f][p, 6].astype(F32) + zfar[f][p, 1].astype(F32)
        if f % 2 == 0:
            two += zfar[f][p, 2].astype(F32)
        else:
            six += zfar[f][p, 2].astype(F32)
        zpart[f][p, 2] = two.astype(BF16)
        zpart[f][p, 6] = six.astype(BF16)
        home_by(-2, 2, 2)
        home_by(2, 6, 3)

    def gathered(p, f):
        arrive(("zn", p, f), znear[f].at[p])
        total = zpart[f][p, 0].astype(F32)
        for i in range(4):
            total += znear[f][p, i].astype(F32)
        return total

    def opposite(f):
        opp[f][0] = gathered(1, f).astype(BF16)
        send(("ob", f), ("ob", f), opp[f].at[0], opp[f].at[1], dev(dx=2), opp[f].at[0])

    def finish(f):
        if f < NF - 1:
            total = gathered(0, f)
        else:
            arrive(("zi", 0, f), zlast)
            total = zpart[f][0, 0].astype(F32)
            for i in range(NZ - 1):
                total += zlast[i].astype(F32)
        arrive(("ob", f), opp[f].at[0])
        total += opp[f][1].astype(F32)
        mine = pl.ds(STARTS[f], WIDTHS[f])
        out[:, mine] = total.astype(BF16)
        pltpu.make_async_copy(out.at[:, mine], out_hbm.at[:, mine], osem.at[0]).start()

    leave(0)
    leave_opposite(0)
    back(1, 0)
    leave(1)
    leave_opposite(1)
    back(1, 1)
    leave(2)
    leave_opposite(2)
    leave(3)
    back(1, 2)
    leave_opposite(3)
    leave(4)
    leave_opposite(4)
    leave(5)
    leave_opposite(5)
    combine(1, 0)
    home(0)
    back(1, 3)
    combine(1, 1)
    closer(1, 0)
    combine(1, 2)
    closer(1, 1)
    home(1)
    back(1, 4)
    opposite(0)
    combine(0, 0)
    closer(1, 2)
    opposite(1)
    combine(1, 3)
    closer(0, 0)
    home(2)
    back(1, 5)
    opposite(2)
    combine(0, 1)
    closer(1, 3)
    combine(1, 4)
    closer(0, 1)
    home(3)
    opposite(3)
    combine(0, 2)
    closer(1, 4)
    combine(1, 5)
    home(4)
    closer(0, 2)
    opposite(4)
    home(5)
    combine(0, 3)
    closer(1, 5)
    combine(0, 4)
    finish(0)
    finish(1)
    closer(0, 3)
    combine(0, 5)
    opposite(5)
    finish(2)
    closer(0, 4)
    finish(3)
    finish(5)
    finish(4)
    sent(list(outward))
    pltpu.make_async_copy(out, out_hbm, osem.at[0]).wait()


def per_device(tokens, routes, route_weights, w_gate, w_up, w_down):
    half = tokens.shape[1]
    hbm = pl.BlockSpec(memory_space=pl.ANY)

    def chunked(*lead):
        return [pltpu.VMEM((*lead, width), BF16) for width in WIDTHS]

    result = pl.pallas_call(
        kernel,
        out_shape=jax.ShapeDtypeStruct((PAD, half), BF16),
        in_specs=[hbm] * 6,
        out_specs=hbm,
        scratch_shapes=[
            pltpu.VMEM((TOK, half), BF16),
            pltpu.VMEM((TOP, TOK), jnp.int32),
            pltpu.VMEM((TOP, TOK), F32),
            pltpu.VMEM((PAD, half), BF16),
            chunked(2, NZ, PAD),
            pltpu.VMEM((2, NZ, PAD, COLS), BF16),
            pltpu.VMEM((2, PLANE, NZ * PAD), BF16),
            pltpu.VMEM((2, NZ * PAD, PLANE), BF16),
            chunked(2, 3, ROWS),
            chunked(2, 4 * PLANE),
            pltpu.VMEM((2 * half, HID), BF16),
            pltpu.VMEM((2 * half, HID), BF16),
            chunked(2 * HID),
            pltpu.VMEM((4 * PLANE, 2 * HID), F32),
            pltpu.VMEM((4 * PLANE, 2 * HID), BF16),
            chunked(4 * PLANE),
            chunked(2, PLANE),
            chunked(2, 3 * ROWS),
            chunked(2, NZ, PAD),
            chunked(2, 3, PAD),
            chunked(2, 4, PAD),
            pltpu.VMEM((NZ - 1, PAD, WIDTHS[-1]), BF16),
            chunked(2, PAD),
            pltpu.SemaphoreType.DMA((3,)),
            pltpu.SemaphoreType.DMA((1,)),
            pltpu.SemaphoreType.DMA((3,)),
            pltpu.SemaphoreType.DMA((51,)),
            pltpu.SemaphoreType.DMA((104,)),
        ],
        compiler_params=pltpu.CompilerParams(
            collective_id=0, has_side_effects=True, vmem_limit_bytes=60 * 1024 * 1024
        ),
        name="experts",
    )(tokens, routes.T, route_weights.T, w_gate, w_up, w_down)
    return result[:TOK]


def solution(mesh):
    placed = (
        P(("attn", "exp"), "rep"),
        P(("attn", "exp"), None),
        P(("attn", "exp"), None),
        P("exp", None, ("attn", "rep")),
        P("exp", None, ("attn", "rep")),
        P("exp", ("attn", "rep"), None),
    )
    return jax.shard_map(
        per_device, mesh=mesh, in_specs=placed, out_specs=P(("attn", "exp"), "rep"), check_vma=False
    )
```

```python
import functools

import jax
import jax.numpy as jnp
from jax import lax
from jax.experimental import pallas as pl
from jax.experimental.pallas import tpu as pltpu
from jax.sharding import PartitionSpec as P

MESH = pl.DeviceIdType.MESH
NX, NZ, NY = 4, 8, 4
WIDTHS = (512, 768, 768, 768, 512, 256)
NF = len(WIDTHS)
STARTS = tuple(sum(WIDTHS[:f]) for f in range(NF))
TOK, PAD, TOP, CAP, HID = 12, 16, 8, 6, 256
COLS = 256
ROWS = NZ * CAP
PLANE = NY * ROWS
F32, BF16 = jnp.float32, jnp.bfloat16


def mm(a, b, dims=((1,), (0,))):
    return lax.dot_general(a, b, (dims, ((), ())), preferred_element_type=F32)


def iota(shape, dim):
    return lax.broadcasted_iota(jnp.int32, shape, dim)


def sixth(n):
    return (n * 10923) >> 16


def kernel(
    tokens_hbm, routes_hbm, weights_hbm, wg_hbm, wu_hbm, wd_hbm, out_hbm,
    tokens, routes, weights, out, tok, tm, pick, mix, ysend, rows, wg, wu, wd, acc, hid,
    part, xback, yback, zpart, zfar, znear, zlast, opp,
    isem, osem, wsem, ssem, rsem,
):
    half = tokens.shape[1]
    x = lax.axis_index("attn")
    e = lax.axis_index("exp")
    c = lax.axis_index("rep")
    z, y = e // NY, lax.rem(e, NY)
    other = 1 - c

    def dev(dx=0, dz=0, dy=0, dc=0):
        return (
            lax.rem(x + dx + NX, NX),
            lax.rem(z + dz + NZ, NZ) * NY + lax.rem(y + dy + NY, NY),
            lax.rem(c + dc, 2),
        )

    partners = [dev(dx=1), dev(dx=-1), dev(dx=2), dev(dc=1)]
    partners += [dev(dy=d) for d in (1, 2, 3)]
    partners += [dev(dz=d) for d in (1, -1, 2, -2, 3, -3, 4)]
    barrier = pltpu.get_barrier_semaphore()
    for partner in partners:
        pl.semaphore_signal(barrier, inc=1, device_id=partner, device_id_type=MESH)

    inputs = [
        pltpu.make_async_copy(src, dst, isem.at[i])
        for i, (src, dst) in enumerate(((tokens_hbm, tokens), (routes_hbm, routes), (weights_hbm, weights)))
    ]
    for copy in inputs:
        copy.start()
    loads = [
        pltpu.make_async_copy(wg_hbm.at[0], wg, wsem.at[0]),
        pltpu.make_async_copy(wu_hbm.at[0], wu, wsem.at[1]),
    ]
    for f in range(NF):
        mine = pl.ds(pl.multiple_of(c * half + STARTS[f], 128), WIDTHS[f])
        loads.append(pltpu.make_async_copy(wd_hbm.at[0, :, mine], wd[f].at[pl.ds(0, HID)], wsem.at[2]))
    narrow = wg.at[pl.ds(0, half)]

    eye = (iota((PAD, TOK), 0) == iota((PAD, TOK), 1)).astype(F32).astype(BF16)

    def placement():
        col = iota((TOK, COLS), 1)
        expert = sixth(col)
        slot = col - CAP * expert
        square = (iota((TOK, TOK), 0) == iota((TOK, TOK), 1)).astype(F32).astype(BF16)
        names = mm(square, routes[...].astype(F32).astype(BF16), ((1,), (1,))).astype(jnp.int32)
        gains = mm(square, weights[...].astype(BF16), ((1,), (1,)))
        hit = jnp.zeros((TOK, COLS), F32)
        weight = jnp.zeros((TOK, COLS), F32)
        for k in range(TOP):
            named = names[:, k:k + 1] == expert
            hit = jnp.where(named, 1.0, hit)
            weight = jnp.where(named, gains[:, k:k + 1], weight)
        lower = (iota((TOK, TOK), 0) > iota((TOK, TOK), 1)).astype(F32).astype(BF16)
        before = mm(lower, hit.astype(BF16))
        placed = jnp.where(before == slot.astype(F32), weight, 0.0)
        tm[0, 0] = mm(eye, placed.astype(BF16)).astype(BF16)

    def padded(f):
        tok[f][0, 0] = mm(eye, tokens[:, STARTS[f]:STARTS[f] + WIDTHS[f]]).astype(BF16)

    inputs[1].wait()
    inputs[2].wait()
    placement()
    inputs[0].wait()
    padded(0)
    padded(1)

    pl.semaphore_wait(barrier, len(partners))

    inward, outward, whole = {}, {}, {}
    free = list(range(ssem.shape[0]))

    def send(out_key, in_key, src, dst, where, block):
        if in_key not in inward:
            inward[in_key] = len(inward)
        if out_key not in outward:
            outward[out_key] = free.pop(0)
            whole[out_key] = block
        pltpu.make_async_remote_copy(
            src_ref=src, dst_ref=dst, send_sem=ssem.at[outward[out_key]], recv_sem=rsem.at[inward[in_key]],
            device_id=where, device_id_type=MESH,
        ).start()

    def waiter(block, sends, arrivals):
        return pltpu.make_async_remote_copy(
            src_ref=block, dst_ref=block, send_sem=ssem.at[sends], recv_sem=rsem.at[arrivals],
            device_id=partners[3], device_id_type=MESH,
        )

    def arrive(key, block):
        waiter(block, 0, inward[key]).wait_recv()

    def sent(keys):
        for key in keys:
            slot = outward.pop(key)
            waiter(whole[key], slot, 0).wait_send()
            free.insert(0, slot)

    hops = ((1, 1, "b"), (-1, 7, "b"), (2, 2, "a"), (-2, 6, "a"))

    def near(p, f):
        if f == 0:
            for s, j, part_of in hops:
                send(("m", p), ("m" + part_of, p), tm.at[p, 0], tm.at[p, j], dev(dz=s), tm.at[p, pl.ds(0, 4)])
        for s, j, part_of in hops:
            send(
                ("z", p, f), ("z" + part_of, p, f), tok[f].at[p, 0], tok[f].at[p, j], dev(dz=s),
                tok[f].at[p, pl.ds(0, 4)],
            )

    def far(p, f):
        if f == 0:
            arrive(("ma", p), tm.at[p, pl.ds(0, 2)])
            for s, i, j in ((1, 2, 3), (-1, 6, 5), (2, 2, 4)):
                send(("mf", p), ("mb", p), tm.at[p, i], tm.at[p, j], dev(dz=s), tm.at[p, pl.ds(0, 3)])
        arrive(("za", p, f), tok[f].at[p, pl.ds(0, 2)])
        for s, i, j in ((1, 2, 3), (-1, 6, 5), (2, 2, 4) if f % 2 == 0 else (-2, 6, 4)):
            send(
                ("zf", p, f), ("zb", p, f), tok[f].at[p, i], tok[f].at[p, j], dev(dz=s),
                tok[f].at[p, pl.ds(0, 3)],
            )

    def matrices(p):
        arrive(("mb", p), tm.at[p, pl.ds(0, 5)])
        table = tm[p].reshape(NZ * PAD, COLS)
        n = iota((PLANE, COLS), 0)
        q = sixth(n)
        want = (z * NY + ((y + (q >> 3)) & 3)) * CAP + (n - CAP * q)
        chosen = (iota((PLANE, COLS), 1) == want).astype(F32).astype(BF16)
        wide = mm(chosen, table, ((1,), (1,)))
        n = iota((PLANE, NZ * PAD), 0)
        keep = (sixth(n) & 7) == (iota((PLANE, NZ * PAD), 1) >> 4)
        pick[p] = jnp.where(keep & (wide != 0.0), 1.0, 0.0).astype(BF16)
        tall = mm(table, chosen, ((1,), (1,)))
        n = iota((NZ * PAD, PLANE), 1)
        keep = (sixth(n) & 7) == (iota((NZ * PAD, PLANE), 0) >> 4)
        mix[p] = jnp.where(keep, tall, 0.0).astype(BF16)

    def base(p):
        return 0 if p == 0 else 3 * PLANE

    def sideways(f, start, size):
        for d, q in ((1, 1), (-1, 2)):
            send(
                ("x", f), ("x", f), rows[f].at[c, pl.ds(start, size)],
                rows[f].at[c, pl.ds(q * PLANE + start, size)], dev(dx=d), rows[f].at[c, pl.ds(PLANE, 2 * PLANE)],
            )

    def choose(p, f):
        if f == 0:
            matrices(p)
        arrive(("zb", p, f), tok[f].at[p, pl.ds(0, 5)])
        got = mm(pick[p], tok[f][p].reshape(NZ * PAD, WIDTHS[f])).astype(BF16)
        rows[f][c, base(p):base(p) + ROWS] = got[:ROWS]
        if p == 0:
            sideways(f, 0, ROWS)
        for d in (1, 2, 3):
            ysend[f][p, d - 1] = got[d * ROWS:(d + 1) * ROWS]
            send(
                ("y", p, f), ("y", p, f), ysend[f].at[p, d - 1],
                rows[f].at[c, pl.ds(base(p) + d * ROWS, ROWS)], dev(dy=d), ysend[f].at[p],
            )

    def to_sibling(f, start, size):
        block = rows[f].at[c, pl.ds(start, size)]
        send(("s", f), ("s", f), block, block, dev(dc=1), rows[f].at[c])

    def from_sibling(f):
        arrive(("s", f), rows[f].at[other])

    def onward(p, f):
        arrive(("y", p, f), rows[f].at[c, pl.ds(base(p) + ROWS, 3 * ROWS)])
        if p == 0:
            sideways(f, ROWS, PLANE - ROWS)
        to_sibling(f, base(p), PLANE)

    def neighbours(f):
        arrive(("x", f), rows[f].at[c, pl.ds(PLANE, 2 * PLANE)])
        to_sibling(f, PLANE, 2 * PLANE)

    def gate_up(f, h):
        depth = pl.ds(pl.multiple_of(h * half + STARTS[f], 128), WIDTHS[f])
        for q in range(2):
            block = rows[f][h, 2 * q * PLANE:2 * (q + 1) * PLANE]
            mine = pl.ds(2 * q * PLANE, 2 * PLANE)
            acc[mine, :HID] += mm(block, wg[depth, :])
            acc[mine, HID:] += mm(block, wu[depth, :])

    items = [(p, f) for p in range(2) for f in range(NF)]
    near(*items[0])
    send(("o", 0), ("om", 0), tm.at[0, 0], tm.at[1, 0], dev(dx=2), tm.at[0, 0])
    near(*items[1])
    for f in range(NF):
        if f > 1:
            padded(f)
        send(("oz",), ("oz",), tok[f].at[0, 0], tok[f].at[1, 0], dev(dx=2), out)
    for load in loads:
        load.start()
    for f in range(NF):
        theirs = pl.ds(pl.multiple_of(other * half + STARTS[f], 128), WIDTHS[f])
        send(("w",), ("w",), wd_hbm.at[0, :, theirs], wd[f].at[pl.ds(HID, HID)], dev(dc=1), narrow)
    acc[...] = jnp.zeros_like(acc)

    def further(step):
        if step < len(items):
            far(*items[step])
        for later in (2, 3) if step == 0 else (step + 3,):
            if later < len(items):
                p, f = items[later]
                if p == 1:
                    if f == 0:
                        arrive(("om", 0), tm.at[0, 0])
                        arrive(("oz",), out)
                near(p, f)

    further(0)
    further(1)
    for step in range(len(items) + 2):
        if step < len(items):
            if step > 0:
                further(step + 2)
            choose(*items[step])
            if step == 0:
                further(2)
        if step >= 2:
            p, f = items[step - 2]
            if p == 1:
                sent([("z", 0, f), ("zf", 0, f), ("y", 0, f)])
            onward(p, f)
            if p == 1:
                neighbours(f)
                if f == 0:
                    loads[0].wait()
                    loads[1].wait()
                gate_up(f, c)
                if f > 0:
                    from_sibling(f - 1)
                    gate_up(f - 1, other)
    sent([key for key in outward if key != ("s", NF - 1)])
    from_sibling(NF - 1)
    gate_up(NF - 1, other)
    inner, outer = pl.ds(PLANE, 2 * PLANE), pl.ds(3 * PLANE, PLANE)
    first = pl.ds(0, PLANE)
    ours, theirs = pl.ds(0, HID), pl.ds(HID, HID)
    for key, mine in (("inner", inner), ("edge", outer), ("edge", first)):
        gate = acc[mine, :HID]
        hid[mine, ours] = (gate / (1.0 + jnp.exp(-gate)) * acc[mine, HID:]).astype(BF16)
        send(("h",), ("h", key), hid.at[mine, ours], hid.at[mine, theirs], dev(dc=1), hid.at[:, ours])

    sent([key for key in outward if key != ("h",)])
    pltpu.make_async_copy(narrow, narrow, wsem.at[2]).wait()
    arrive(("w",), narrow)
    arrive(("h", "inner"), hid.at[inner, theirs])

    def down(f, mine):
        part[f][mine] = mm(hid[mine], wd[f][...]).astype(BF16)

    def leave(f):
        down(f, inner)
        for d, q, place in ((-1, 1, 1), (1, 2, 0)):
            send(
                ("xb", f), ("xb", f), part[f].at[pl.ds(q * PLANE, PLANE)], xback[f].at[place], dev(dx=d), xback[f]
            )

    def leave_opposite(f):
        if f == 0:
            arrive(("h", "edge"), hid.at[inner, theirs])
        down(f, outer)
        down(f, first)

    def back(p, f):
        for d in (1, 2, 3):
            send(
                ("yb", p, f), ("yb", p, f), part[f].at[pl.ds(base(p) + d * ROWS, ROWS)],
                yback[f].at[p, pl.ds((d - 1) * ROWS, ROWS)], dev(dy=-d), yback[f].at[p],
            )

    def home(f):
        arrive(("xb", f), xback[f])
        total = part[f][first].astype(F32) + xback[f][0].astype(F32) + xback[f][1].astype(F32)
        part[f][first] = total.astype(BF16)
        back(0, f)

    def combine(p, f):
        arrive(("yb", p, f), yback[f].at[p])
        total = mm(mix[p, :, :ROWS], part[f][base(p):base(p) + ROWS])
        total += mm(mix[p, :, ROWS:], yback[f][p])
        zpart[f][p] = total.astype(BF16).reshape(NZ, PAD, WIDTHS[f])
        if (p, f) == (0, NF - 1):
            for j in range(1, NZ):
                send(("zi", p, f), ("zi", p, f), zpart[f].at[p, j], zlast.at[j - 1], dev(dz=-j), zlast)
            return
        for s, j, place in ((-1, 3, 0), (1, 5, 1), (-2 if f % 2 == 0 else 2, 4, 2)):
            send(("zi", p, f), ("zi", p, f), zpart[f].at[p, j], zfar[f].at[p, place], dev(dz=s), zfar[f].at[p])

    def closer(p, f):
        def home_by(s, j, place):
            send(("zn", p, f), ("zn", p, f), zpart[f].at[p, j], znear[f].at[p, place], dev(dz=s), znear[f].at[p])

        home_by(-1, 1, 0)
        home_by(1, 7, 1)
        arrive(("zi", p, f), zfar[f].at[p])
        two = zpart[f][p, 2].astype(F32) + zfar[f][p, 0].astype(F32)
        six = zpart[f][p, 6].astype(F32) + zfar[f][p, 1].astype(F32)
        if f % 2 == 0:
            two += zfar[f][p, 2].astype(F32)
        else:
            six += zfar[f][p, 2].astype(F32)
        zpart[f][p, 2] = two.astype(BF16)
        zpart[f][p, 6] = six.astype(BF16)
        home_by(-2, 2, 2)
        home_by(2, 6, 3)

    def gathered(p, f):
        arrive(("zn", p, f), znear[f].at[p])
        total = zpart[f][p, 0].astype(F32)
        for i in range(4):
            total += znear[f][p, i].astype(F32)
        return total

    def opposite(f):
        opp[f][0] = gathered(1, f).astype(BF16)
        send(("ob", f), ("ob", f), opp[f].at[0], opp[f].at[1], dev(dx=2), opp[f].at[0])

    def finish(f):
        if f < NF - 1:
            total = gathered(0, f)
        else:
            arrive(("zi", 0, f), zlast)
            total = zpart[f][0, 0].astype(F32)
            for i in range(NZ - 1):
                total += zlast[i].astype(F32)
        arrive(("ob", f), opp[f].at[0])
        total += opp[f][1].astype(F32)
        mine = pl.ds(STARTS[f], WIDTHS[f])
        out[:, mine] = total.astype(BF16)
        pltpu.make_async_copy(out.at[:, mine], out_hbm.at[:, mine], osem.at[0]).start()

    leave(0)
    leave(1)
    leave_opposite(0)
    leave(2)
    back(1, 0)
    leave(3)
    leave_opposite(1)
    back(1, 1)
    leave_opposite(3)
    leave_opposite(2)
    leave(4)
    back(1, 2)
    combine(1, 0)
    leave(5)
    back(1, 3)
    home(0)
    leave_opposite(5)
    combine(1, 1)
    combine(1, 2)
    closer(1, 1)
    closer(1, 0)
    home(1)
    combine(1, 3)
    back(1, 5)
    closer(1, 2)
    combine(0, 0)
    home(2)
    closer(1, 3)
    leave_opposite(4)
    back(1, 4)
    combine(1, 5)
    opposite(2)
    combine(0, 1)
    home(3)
    combine(0, 2)
    closer(0, 0)
    combine(1, 4)
    closer(0, 1)
    home(4)
    closer(1, 5)
    opposite(0)
    closer(0, 2)
    home(5)
    opposite(1)
    combine(0, 3)
    closer(1, 4)
    combine(0, 4)
    finish(0)
    opposite(3)
    opposite(5)
    combine(0, 5)
    finish(1)
    closer(0, 3)
    finish(2)
    closer(0, 4)
    opposite(4)
    finish(3)
    finish(5)
    finish(4)
    sent(list(outward))
    pltpu.make_async_copy(out, out_hbm, osem.at[0]).wait()


def per_device(tokens, routes, route_weights, w_gate, w_up, w_down):
    half = tokens.shape[1]
    hbm = pl.BlockSpec(memory_space=pl.ANY)

    def chunked(*lead):
        return [pltpu.VMEM((*lead, width), BF16) for width in WIDTHS]

    result = pl.pallas_call(
        kernel,
        out_shape=jax.ShapeDtypeStruct((PAD, half), BF16),
        in_specs=[hbm] * 6,
        out_specs=hbm,
        scratch_shapes=[
            pltpu.VMEM((TOK, half), BF16),
            pltpu.VMEM((TOP, TOK), jnp.int32),
            pltpu.VMEM((TOP, TOK), F32),
            pltpu.VMEM((PAD, half), BF16),
            chunked(2, NZ, PAD),
            pltpu.VMEM((2, NZ, PAD, COLS), BF16),
            pltpu.VMEM((2, PLANE, NZ * PAD), BF16),
            pltpu.VMEM((2, NZ * PAD, PLANE), BF16),
            chunked(2, 3, ROWS),
            chunked(2, 4 * PLANE),
            pltpu.VMEM((2 * half, HID), BF16),
            pltpu.VMEM((2 * half, HID), BF16),
            chunked(2 * HID),
            pltpu.VMEM((4 * PLANE, 2 * HID), F32),
            pltpu.VMEM((4 * PLANE, 2 * HID), BF16),
            chunked(4 * PLANE),
            chunked(2, PLANE),
            chunked(2, 3 * ROWS),
            chunked(2, NZ, PAD),
            chunked(2, 3, PAD),
            chunked(2, 4, PAD),
            pltpu.VMEM((NZ - 1, PAD, WIDTHS[-1]), BF16),
            chunked(2, PAD),
            pltpu.SemaphoreType.DMA((3,)),
            pltpu.SemaphoreType.DMA((1,)),
            pltpu.SemaphoreType.DMA((3,)),
            pltpu.SemaphoreType.DMA((51,)),
            pltpu.SemaphoreType.DMA((104,)),
        ],
        compiler_params=pltpu.CompilerParams(
            collective_id=0, has_side_effects=True, vmem_limit_bytes=60 * 1024 * 1024
        ),
        name="experts",
    )(tokens, routes.T, route_weights.T, w_gate, w_up, w_down)
    return result[:TOK]


def solution(mesh):
    placed = (
        P(("attn", "exp"), "rep"),
        P(("attn", "exp"), None),
        P(("attn", "exp"), None),
        P("exp", None, ("attn", "rep")),
        P("exp", None, ("attn", "rep")),
        P("exp", ("attn", "rep"), None),
    )
    return jax.shard_map(
        per_device, mesh=mesh, in_specs=placed, out_specs=P(("attn", "exp"), "rep"), check_vma=False
    )
```

```python
import functools

import jax
import jax.numpy as jnp
from jax import lax
from jax.experimental import pallas as pl
from jax.experimental.pallas import tpu as pltpu
from jax.sharding import PartitionSpec as P

MESH = pl.DeviceIdType.MESH
NX, NZ, NY = 4, 8, 4
WIDTHS = (512, 768, 768, 768, 512, 256)
NF = len(WIDTHS)
STARTS = tuple(sum(WIDTHS[:f]) for f in range(NF))
TOK, PAD, TOP, CAP, HID = 12, 16, 8, 6, 256
COLS = 256
ROWS = NZ * CAP
PLANE = NY * ROWS
F32, BF16 = jnp.float32, jnp.bfloat16


def mm(a, b, dims=((1,), (0,))):
    return lax.dot_general(a, b, (dims, ((), ())), preferred_element_type=F32)


def iota(shape, dim):
    return lax.broadcasted_iota(jnp.int32, shape, dim)


def sixth(n):
    return (n * 10923) >> 16


def kernel(
    tokens_hbm, routes_hbm, weights_hbm, wg_hbm, wu_hbm, wd_hbm, out,
    tokens, routes, weights, tok, tm, pick, mix, ysend, rows, wg, wu, wd, acc, hid,
    part, xback, yback, zpart, zfar, znear, zlast, opp,
    isem, wsem, ssem, rsem,
):
    half = tokens.shape[1]
    x = lax.axis_index("attn")
    e = lax.axis_index("exp")
    c = lax.axis_index("rep")
    z, y = e // NY, lax.rem(e, NY)
    other = 1 - c

    def dev(dx=0, dz=0, dy=0, dc=0):
        return (
            lax.rem(x + dx + NX, NX),
            lax.rem(z + dz + NZ, NZ) * NY + lax.rem(y + dy + NY, NY),
            lax.rem(c + dc, 2),
        )

    partners = [dev(dx=1), dev(dx=-1), dev(dx=2), dev(dc=1)]
    partners += [dev(dy=d) for d in (1, 2, 3)]
    partners += [dev(dz=d) for d in (1, -1, 2, -2, 3, -3, 4)]
    barrier = pltpu.get_barrier_semaphore()
    for partner in partners:
        pl.semaphore_signal(barrier, inc=1, device_id=partner, device_id_type=MESH)

    inputs = [
        pltpu.make_async_copy(src, dst, isem.at[i])
        for i, (src, dst) in enumerate(((tokens_hbm, tokens), (routes_hbm, routes), (weights_hbm, weights)))
    ]
    for copy in inputs:
        copy.start()
    loads = [
        pltpu.make_async_copy(wg_hbm.at[0], wg, wsem.at[0]),
        pltpu.make_async_copy(wu_hbm.at[0], wu, wsem.at[1]),
    ]
    for f in range(NF):
        mine = pl.ds(pl.multiple_of(c * half + STARTS[f], 128), WIDTHS[f])
        loads.append(pltpu.make_async_copy(wd_hbm.at[0, :, mine], wd[f].at[pl.ds(0, HID)], wsem.at[2]))
    narrow = wg.at[pl.ds(0, half)]

    eye = (iota((PAD, TOK), 0) == iota((PAD, TOK), 1)).astype(F32).astype(BF16)

    def placement():
        col = iota((TOK, COLS), 1)
        expert = sixth(col)
        slot = col - CAP * expert
        square = (iota((TOK, TOK), 0) == iota((TOK, TOK), 1)).astype(F32).astype(BF16)
        names = mm(square, routes[...].astype(F32).astype(BF16), ((1,), (1,))).astype(jnp.int32)
        gains = mm(square, weights[...].astype(BF16), ((1,), (1,)))
        hit = jnp.zeros((TOK, COLS), F32)
        weight = jnp.zeros((TOK, COLS), F32)
        for k in range(TOP):
            named = names[:, k:k + 1] == expert
            hit = jnp.where(named, 1.0, hit)
            weight = jnp.where(named, gains[:, k:k + 1], weight)
        lower = (iota((TOK, TOK), 0) > iota((TOK, TOK), 1)).astype(F32).astype(BF16)
        before = mm(lower, hit.astype(BF16))
        placed = jnp.where(before == slot.astype(F32), weight, 0.0)
        tm[0, 0] = mm(eye, placed.astype(BF16)).astype(BF16)

    def padded(f):
        tok[f][0, 0] = mm(eye, tokens[:, STARTS[f]:STARTS[f] + WIDTHS[f]]).astype(BF16)

    inputs[1].wait()
    inputs[2].wait()
    placement()
    inputs[0].wait()
    padded(0)
    padded(1)

    pl.semaphore_wait(barrier, len(partners))

    inward, outward, whole = {}, {}, {}
    free = list(range(ssem.shape[0]))

    def send(out_key, in_key, src, dst, where, block):
        if in_key not in inward:
            inward[in_key] = len(inward)
        if out_key not in outward:
            outward[out_key] = free.pop(0)
            whole[out_key] = block
        pltpu.make_async_remote_copy(
            src_ref=src, dst_ref=dst, send_sem=ssem.at[outward[out_key]], recv_sem=rsem.at[inward[in_key]],
            device_id=where, device_id_type=MESH,
        ).start()

    def waiter(block, sends, arrivals):
        return pltpu.make_async_remote_copy(
            src_ref=block, dst_ref=block, send_sem=ssem.at[sends], recv_sem=rsem.at[arrivals],
            device_id=partners[3], device_id_type=MESH,
        )

    def arrive(key, block):
        waiter(block, 0, inward[key]).wait_recv()

    def sent(keys):
        for key in keys:
            slot = outward.pop(key)
            waiter(whole[key], slot, 0).wait_send()
            free.insert(0, slot)

    hops = ((1, 1, "b"), (-1, 7, "b"), (2, 2, "a"), (-2, 6, "a"))

    def near(p, f):
        if f == 0:
            for s, j, part_of in hops:
                send(("m", p), ("m" + part_of, p), tm.at[p, 0], tm.at[p, j], dev(dz=s), tm.at[p, pl.ds(0, 4)])
        for s, j, part_of in hops:
            send(
                ("z", p, f), ("z" + part_of, p, f), tok[f].at[p, 0], tok[f].at[p, j], dev(dz=s),
                tok[f].at[p, pl.ds(0, 4)],
            )

    def far(p, f):
        if f == 0:
            arrive(("ma", p), tm.at[p, pl.ds(0, 2)])
            for s, i, j in ((1, 2, 3), (-1, 6, 5), (2, 2, 4)):
                send(("mf", p), ("mb", p), tm.at[p, i], tm.at[p, j], dev(dz=s), tm.at[p, pl.ds(0, 3)])
        arrive(("za", p, f), tok[f].at[p, pl.ds(0, 2)])
        for s, i, j in ((1, 2, 3), (-1, 6, 5), (2, 2, 4) if f % 2 == 0 else (-2, 6, 4)):
            send(
                ("zf", p, f), ("zb", p, f), tok[f].at[p, i], tok[f].at[p, j], dev(dz=s),
                tok[f].at[p, pl.ds(0, 3)],
            )

    def matrices(p):
        arrive(("mb", p), tm.at[p, pl.ds(0, 5)])
        table = tm[p].reshape(NZ * PAD, COLS)
        n = iota((PLANE, COLS), 0)
        q = sixth(n)
        want = (z * NY + ((y + (q >> 3)) & 3)) * CAP + (n - CAP * q)
        chosen = (iota((PLANE, COLS), 1) == want).astype(F32).astype(BF16)
        wide = mm(chosen, table, ((1,), (1,)))
        n = iota((PLANE, NZ * PAD), 0)
        keep = (sixth(n) & 7) == (iota((PLANE, NZ * PAD), 1) >> 4)
        pick[p] = jnp.where(keep & (wide != 0.0), 1.0, 0.0).astype(BF16)
        tall = mm(table, chosen, ((1,), (1,)))
        n = iota((NZ * PAD, PLANE), 1)
        keep = (sixth(n) & 7) == (iota((NZ * PAD, PLANE), 0) >> 4)
        mix[p] = jnp.where(keep, tall, 0.0).astype(BF16)

    def base(p):
        return 0 if p == 0 else 3 * PLANE

    def sideways(f, start, size):
        for d, q in ((1, 1), (-1, 2)):
            send(
                ("x", f), ("x", f), rows[f].at[c, pl.ds(start, size)],
                rows[f].at[c, pl.ds(q * PLANE + start, size)], dev(dx=d), rows[f].at[c, pl.ds(PLANE, 2 * PLANE)],
            )

    def choose(p, f):
        if f == 0:
            matrices(p)
        arrive(("zb", p, f), tok[f].at[p, pl.ds(0, 5)])
        got = mm(pick[p], tok[f][p].reshape(NZ * PAD, WIDTHS[f])).astype(BF16)
        rows[f][c, base(p):base(p) + ROWS] = got[:ROWS]
        if p == 0:
            sideways(f, 0, ROWS)
        for d in (1, 2, 3):
            ysend[f][p, d - 1] = got[d * ROWS:(d + 1) * ROWS]
            send(
                ("y", p, f), ("y", p, f), ysend[f].at[p, d - 1],
                rows[f].at[c, pl.ds(base(p) + d * ROWS, ROWS)], dev(dy=d), ysend[f].at[p],
            )

    def to_sibling(f, start, size):
        block = rows[f].at[c, pl.ds(start, size)]
        send(("s", f), ("s", f), block, block, dev(dc=1), rows[f].at[c])

    def from_sibling(f):
        arrive(("s", f), rows[f].at[other])

    def onward(p, f):
        arrive(("y", p, f), rows[f].at[c, pl.ds(base(p) + ROWS, 3 * ROWS)])
        if p == 0:
            sideways(f, ROWS, PLANE - ROWS)
        to_sibling(f, base(p), PLANE)

    def neighbours(f):
        arrive(("x", f), rows[f].at[c, pl.ds(PLANE, 2 * PLANE)])
        to_sibling(f, PLANE, 2 * PLANE)

    def gate_up(f, h):
        depth = pl.ds(pl.multiple_of(h * half + STARTS[f], 128), WIDTHS[f])
        for q in range(2):
            block = rows[f][h, 2 * q * PLANE:2 * (q + 1) * PLANE]
            mine = pl.ds(2 * q * PLANE, 2 * PLANE)
            acc[mine, :HID] += mm(block, wg[depth, :])
            acc[mine, HID:] += mm(block, wu[depth, :])

    items = [(p, f) for p in range(2) for f in range(NF)]
    near(*items[0])
    send(("o", 0), ("om", 0), tm.at[0, 0], tm.at[1, 0], dev(dx=2), tm.at[0, 0])
    near(*items[1])
    for f in range(NF):
        if f > 1:
            padded(f)
        send(("oz",), ("oz",), tok[f].at[0, 0], tok[f].at[1, 0], dev(dx=2), out)
    for load in loads:
        load.start()
    for f in range(NF):
        theirs = pl.ds(pl.multiple_of(other * half + STARTS[f], 128), WIDTHS[f])
        send(("w",), ("w",), wd_hbm.at[0, :, theirs], wd[f].at[pl.ds(HID, HID)], dev(dc=1), narrow)
    acc[...] = jnp.zeros_like(acc)

    def further(step):
        if step < len(items):
            far(*items[step])
        for later in {0: (2,), 1: (3, 4)}.get(step, (step + 3,)):
            if later < len(items):
                p, f = items[later]
                if p == 1:
                    if f == 0:
                        arrive(("om", 0), tm.at[0, 0])
                        arrive(("oz",), out)
                near(p, f)

    further(0)
    further(1)
    for step in range(len(items) + 2):
        if step < len(items):
            if step > 0:
                further(step + 2)
            choose(*items[step])
            if step == 0:
                further(2)
        if step >= 2:
            p, f = items[step - 2]
            if p == 1:
                sent([("z", 0, f), ("zf", 0, f), ("y", 0, f)])
            onward(p, f)
            if p == 1:
                neighbours(f)
                if f == 0:
                    loads[0].wait()
                    loads[1].wait()
                gate_up(f, c)
                if f > 0:
                    from_sibling(f - 1)
                    gate_up(f - 1, other)
    sent([key for key in outward if key != ("s", NF - 1)])
    from_sibling(NF - 1)
    gate_up(NF - 1, other)
    inner, outer = pl.ds(PLANE, 2 * PLANE), pl.ds(3 * PLANE, PLANE)
    first = pl.ds(0, PLANE)
    ours, theirs = pl.ds(0, HID), pl.ds(HID, HID)
    for key, mine in (("inner", inner), ("edge", outer), ("edge", first)):
        gate = acc[mine, :HID]
        hid[mine, ours] = (gate / (1.0 + jnp.exp(-gate)) * acc[mine, HID:]).astype(BF16)
        send(("h",), ("h", key), hid.at[mine, ours], hid.at[mine, theirs], dev(dc=1), hid.at[:, ours])

    sent([key for key in outward if key != ("h",)])
    pltpu.make_async_copy(narrow, narrow, wsem.at[2]).wait()
    arrive(("w",), narrow)
    arrive(("h", "inner"), hid.at[inner, theirs])

    def down(f, mine):
        part[f][mine] = mm(hid[mine], wd[f][...]).astype(BF16)

    def leave(f):
        down(f, inner)
        for d, q, place in ((-1, 1, 1), (1, 2, 0)):
            send(
                ("xb", f), ("xb", f), part[f].at[pl.ds(q * PLANE, PLANE)], xback[f].at[place], dev(dx=d), xback[f]
            )

    def leave_opposite(f):
        if f == 0:
            arrive(("h", "edge"), hid.at[inner, theirs])
        down(f, outer)
        down(f, first)

    def back(p, f):
        for d in (1, 2, 3):
            send(
                ("yb", p, f), ("yb", p, f), part[f].at[pl.ds(base(p) + d * ROWS, ROWS)],
                yback[f].at[p, pl.ds((d - 1) * ROWS, ROWS)], dev(dy=-d), yback[f].at[p],
            )

    def home(f):
        arrive(("xb", f), xback[f])
        total = part[f][first].astype(F32) + xback[f][0].astype(F32) + xback[f][1].astype(F32)
        part[f][first] = total.astype(BF16)
        back(0, f)

    def combine(p, f):
        arrive(("yb", p, f), yback[f].at[p])
        total = mm(mix[p, :, :ROWS], part[f][base(p):base(p) + ROWS])
        total += mm(mix[p, :, ROWS:], yback[f][p])
        zpart[f][p] = total.astype(BF16).reshape(NZ, PAD, WIDTHS[f])
        if (p, f) == (0, NF - 1):
            for j in range(1, NZ):
                send(("zi", p, f), ("zi", p, f), zpart[f].at[p, j], zlast.at[j - 1], dev(dz=-j), zlast)
            return
        for s, j, place in ((-1, 3, 0), (1, 5, 1), (-2 if f % 2 == 0 else 2, 4, 2)):
            send(("zi", p, f), ("zi", p, f), zpart[f].at[p, j], zfar[f].at[p, place], dev(dz=s), zfar[f].at[p])

    def closer(p, f):
        def home_by(s, j, place):
            send(("zn", p, f), ("zn", p, f), zpart[f].at[p, j], znear[f].at[p, place], dev(dz=s), znear[f].at[p])

        home_by(-1, 1, 0)
        home_by(1, 7, 1)
        arrive(("zi", p, f), zfar[f].at[p])
        two = zpart[f][p, 2].astype(F32) + zfar[f][p, 0].astype(F32)
        six = zpart[f][p, 6].astype(F32) + zfar[f][p, 1].astype(F32)
        if f % 2 == 0:
            two += zfar[f][p, 2].astype(F32)
        else:
            six += zfar[f][p, 2].astype(F32)
        zpart[f][p, 2] = two.astype(BF16)
        zpart[f][p, 6] = six.astype(BF16)
        home_by(-2, 2, 2)
        home_by(2, 6, 3)

    def gathered(p, f):
        arrive(("zn", p, f), znear[f].at[p])
        total = zpart[f][p, 0].astype(F32)
        for i in range(4):
            total += znear[f][p, i].astype(F32)
        return total

    def opposite(f):
        opp[f][0] = gathered(1, f).astype(BF16)
        send(("ob", f), ("ob", f), opp[f].at[0], opp[f].at[1], dev(dx=2), opp[f].at[0])

    def finish(f):
        if f < NF - 1:
            total = gathered(0, f)
        else:
            arrive(("zi", 0, f), zlast)
            total = zpart[f][0, 0].astype(F32)
            for i in range(NZ - 1):
                total += zlast[i].astype(F32)
        arrive(("ob", f), opp[f].at[0])
        total += opp[f][1].astype(F32)
        mine = pl.ds(STARTS[f], WIDTHS[f])
        out[:, mine] = total.astype(BF16)

    leave(0)
    leave(1)
    leave_opposite(0)
    leave(2)
    back(1, 0)
    leave(3)
    leave_opposite(1)
    back(1, 1)
    leave_opposite(3)
    leave_opposite(2)
    leave(4)
    back(1, 2)
    combine(1, 0)
    leave(5)
    back(1, 3)
    home(0)
    leave_opposite(5)
    combine(1, 1)
    combine(1, 2)
    closer(1, 1)
    closer(1, 0)
    home(1)
    combine(1, 3)
    back(1, 5)
    closer(1, 2)
    combine(0, 0)
    home(2)
    closer(1, 3)
    leave_opposite(4)
    back(1, 4)
    combine(1, 5)
    opposite(2)
    combine(0, 1)
    home(3)
    combine(0, 2)
    closer(0, 0)
    combine(1, 4)
    closer(0, 1)
    home(4)
    closer(1, 5)
    opposite(0)
    closer(0, 2)
    home(5)
    opposite(1)
    combine(0, 3)
    closer(1, 4)
    combine(0, 4)
    finish(0)
    opposite(3)
    opposite(5)
    combine(0, 5)
    finish(1)
    closer(0, 3)
    finish(2)
    closer(0, 4)
    opposite(4)
    finish(3)
    finish(5)
    finish(4)
    sent(list(outward))


def per_device(tokens, routes, route_weights, w_gate, w_up, w_down):
    half = tokens.shape[1]
    hbm = pl.BlockSpec(memory_space=pl.ANY)

    def chunked(*lead):
        return [pltpu.VMEM((*lead, width), BF16) for width in WIDTHS]

    result = pl.pallas_call(
        kernel,
        out_shape=pltpu.VMEM((PAD, half), BF16),
        in_specs=[hbm] * 6,
        out_specs=pl.BlockSpec(memory_space=pltpu.VMEM),
        scratch_shapes=[
            pltpu.VMEM((TOK, half), BF16),
            pltpu.VMEM((TOP, TOK), jnp.int32),
            pltpu.VMEM((TOP, TOK), F32),
            chunked(2, NZ, PAD),
            pltpu.VMEM((2, NZ, PAD, COLS), BF16),
            pltpu.VMEM((2, PLANE, NZ * PAD), BF16),
            pltpu.VMEM((2, NZ * PAD, PLANE), BF16),
            chunked(2, 3, ROWS),
            chunked(2, 4 * PLANE),
            pltpu.VMEM((2 * half, HID), BF16),
            pltpu.VMEM((2 * half, HID), BF16),
            chunked(2 * HID),
            pltpu.VMEM((4 * PLANE, 2 * HID), F32),
            pltpu.VMEM((4 * PLANE, 2 * HID), BF16),
            chunked(4 * PLANE),
            chunked(2, PLANE),
            chunked(2, 3 * ROWS),
            chunked(2, NZ, PAD),
            chunked(2, 3, PAD),
            chunked(2, 4, PAD),
            pltpu.VMEM((NZ - 1, PAD, WIDTHS[-1]), BF16),
            chunked(2, PAD),
            pltpu.SemaphoreType.DMA((3,)),
            pltpu.SemaphoreType.DMA((3,)),
            pltpu.SemaphoreType.DMA((51,)),
            pltpu.SemaphoreType.DMA((104,)),
        ],
        compiler_params=pltpu.CompilerParams(
            collective_id=0, has_side_effects=True, vmem_limit_bytes=60 * 1024 * 1024
        ),
        name="experts",
    )(tokens, routes.T, route_weights.T, w_gate, w_up, w_down)
    return result[:TOK]


def solution(mesh):
    placed = (
        P(("attn", "exp"), "rep"),
        P(("attn", "exp"), None),
        P(("attn", "exp"), None),
        P("exp", None, ("attn", "rep")),
        P("exp", None, ("attn", "rep")),
        P("exp", ("attn", "rep"), None),
    )
    return jax.shard_map(
        per_device, mesh=mesh, in_specs=placed, out_specs=P(("attn", "exp"), "rep"), check_vma=False
    )
```

```python
import functools

import jax
import jax.numpy as jnp
from jax import lax
from jax.experimental import pallas as pl
from jax.experimental.pallas import tpu as pltpu
from jax.sharding import PartitionSpec as P

MESH = pl.DeviceIdType.MESH
NX, NZ, NY = 4, 8, 4
WIDTHS = (512, 768, 768, 768, 512, 256)
NF = len(WIDTHS)
STARTS = tuple(sum(WIDTHS[:f]) for f in range(NF))
TOK, PAD, TOP, CAP, HID = 12, 16, 8, 6, 256
COLS = 256
ROWS = NZ * CAP
PLANE = NY * ROWS
F32, BF16 = jnp.float32, jnp.bfloat16


def mm(a, b, dims=((1,), (0,))):
    return lax.dot_general(a, b, (dims, ((), ())), preferred_element_type=F32)


def iota(shape, dim):
    return lax.broadcasted_iota(jnp.int32, shape, dim)


def sixth(n):
    return (n * 10923) >> 16


def kernel(
    tokens_hbm, routes_hbm, weights_hbm, wg_hbm, wu_hbm, wd_hbm, out,
    tokens, routes, weights, tok, tm, pick, mix, ysend, rows, wg, wu, wd, acc, hid,
    part, xback, yback, zpart, zfar, znear, zlast, opp,
    isem, wsem, ssem, rsem,
):
    half = tokens.shape[1]
    x = lax.axis_index("attn")
    e = lax.axis_index("exp")
    c = lax.axis_index("rep")
    z, y = e // NY, lax.rem(e, NY)
    other = 1 - c

    def dev(dx=0, dz=0, dy=0, dc=0):
        return (
            lax.rem(x + dx + NX, NX),
            lax.rem(z + dz + NZ, NZ) * NY + lax.rem(y + dy + NY, NY),
            lax.rem(c + dc, 2),
        )

    partners = [dev(dx=1), dev(dx=-1), dev(dx=2), dev(dc=1)]
    partners += [dev(dy=d) for d in (1, 2, 3)]
    partners += [dev(dz=d) for d in (1, -1, 2, -2, 3, -3, 4)]
    barrier = pltpu.get_barrier_semaphore()
    for partner in partners:
        pl.semaphore_signal(barrier, inc=1, device_id=partner, device_id_type=MESH)

    inputs = [
        pltpu.make_async_copy(src, dst, isem.at[i])
        for i, (src, dst) in enumerate(((tokens_hbm, tokens), (routes_hbm, routes), (weights_hbm, weights)))
    ]
    for copy in inputs:
        copy.start()
    loads = [
        pltpu.make_async_copy(wg_hbm.at[0], wg, wsem.at[0]),
        pltpu.make_async_copy(wu_hbm.at[0], wu, wsem.at[1]),
    ]
    for f in range(NF):
        mine = pl.ds(pl.multiple_of(c * half + STARTS[f], 128), WIDTHS[f])
        loads.append(pltpu.make_async_copy(wd_hbm.at[0, :, mine], wd[f].at[pl.ds(0, HID)], wsem.at[2]))
    narrow = wg.at[pl.ds(0, half)]

    eye = (iota((PAD, TOK), 0) == iota((PAD, TOK), 1)).astype(F32).astype(BF16)

    def placement():
        col = iota((TOK, COLS), 1)
        expert = sixth(col)
        slot = col - CAP * expert
        square = (iota((TOK, TOK), 0) == iota((TOK, TOK), 1)).astype(F32).astype(BF16)
        names = mm(square, routes[...].astype(F32).astype(BF16), ((1,), (1,))).astype(jnp.int32)
        gains = mm(square, weights[...].astype(BF16), ((1,), (1,)))
        hit = jnp.zeros((TOK, COLS), F32)
        weight = jnp.zeros((TOK, COLS), F32)
        for k in range(TOP):
            named = names[:, k:k + 1] == expert
            hit = jnp.where(named, 1.0, hit)
            weight = jnp.where(named, gains[:, k:k + 1], weight)
        lower = (iota((TOK, TOK), 0) > iota((TOK, TOK), 1)).astype(F32).astype(BF16)
        before = mm(lower, hit.astype(BF16))
        placed = jnp.where(before == slot.astype(F32), weight, 0.0)
        tm[0, 0] = mm(eye, placed.astype(BF16)).astype(BF16)

    def padded(f):
        tok[f][0, 0] = mm(eye, tokens[:, STARTS[f]:STARTS[f] + WIDTHS[f]]).astype(BF16)

    inputs[1].wait()
    inputs[2].wait()
    placement()
    inputs[0].wait()
    padded(0)

    pl.semaphore_wait(barrier, len(partners))

    inward, outward, whole = {}, {}, {}
    free = list(range(ssem.shape[0]))

    def send(out_key, in_key, src, dst, where, block):
        if in_key not in inward:
            inward[in_key] = len(inward)
        if out_key not in outward:
            outward[out_key] = free.pop(0)
            whole[out_key] = block
        pltpu.make_async_remote_copy(
            src_ref=src, dst_ref=dst, send_sem=ssem.at[outward[out_key]], recv_sem=rsem.at[inward[in_key]],
            device_id=where, device_id_type=MESH,
        ).start()

    def waiter(block, sends, arrivals):
        return pltpu.make_async_remote_copy(
            src_ref=block, dst_ref=block, send_sem=ssem.at[sends], recv_sem=rsem.at[arrivals],
            device_id=partners[3], device_id_type=MESH,
        )

    def arrive(key, block):
        waiter(block, 0, inward[key]).wait_recv()

    def sent(keys):
        for key in keys:
            slot = outward.pop(key)
            waiter(whole[key], slot, 0).wait_send()
            free.insert(0, slot)

    hops = ((1, 1, "b"), (-1, 7, "b"), (2, 2, "a"), (-2, 6, "a"))

    def near(p, f):
        if f == 0:
            for s, j, part_of in hops:
                send(("m", p), ("m" + part_of, p), tm.at[p, 0], tm.at[p, j], dev(dz=s), tm.at[p, pl.ds(0, 7)])
        for s, j, part_of in hops:
            send(
                ("z", p, f), ("z" + part_of, p, f), tok[f].at[p, 0], tok[f].at[p, j], dev(dz=s),
                tok[f].at[p, pl.ds(0, 7)],
            )

    def far(p, f):
        if f == 0:
            arrive(("ma", p), tm.at[p, pl.ds(0, 2)])
            for s, i, j in ((1, 2, 3), (-1, 6, 5), (2, 2, 4)):
                send(("m", p), ("mb", p), tm.at[p, i], tm.at[p, j], dev(dz=s), tm.at[p, pl.ds(0, 7)])
        arrive(("za", p, f), tok[f].at[p, pl.ds(0, 2)])
        for s, i, j in ((1, 2, 3), (-1, 6, 5), (2, 2, 4) if f % 2 == 0 else (-2, 6, 4)):
            send(
                ("z", p, f), ("zb", p, f), tok[f].at[p, i], tok[f].at[p, j], dev(dz=s),
                tok[f].at[p, pl.ds(0, 7)],
            )

    def matrices(p):
        arrive(("mb", p), tm.at[p, pl.ds(0, 5)])
        table = tm[p].reshape(NZ * PAD, COLS)
        n = iota((PLANE, COLS), 0)
        q = sixth(n)
        want = (z * NY + ((y + (q >> 3)) & 3)) * CAP + (n - CAP * q)
        chosen = (iota((PLANE, COLS), 1) == want).astype(F32).astype(BF16)
        wide = mm(chosen, table, ((1,), (1,)))
        n = iota((PLANE, NZ * PAD), 0)
        keep = (sixth(n) & 7) == (iota((PLANE, NZ * PAD), 1) >> 4)
        pick[p] = jnp.where(keep & (wide != 0.0), 1.0, 0.0).astype(BF16)
        tall = mm(table, chosen, ((1,), (1,)))
        n = iota((NZ * PAD, PLANE), 1)
        keep = (sixth(n) & 7) == (iota((NZ * PAD, PLANE), 0) >> 4)
        mix[p] = jnp.where(keep, tall, 0.0).astype(BF16)

    def base(p):
        return 0 if p == 0 else 3 * PLANE

    def sideways(f, start, size):
        for d, q in ((1, 1), (-1, 2)):
            send(
                ("x", f), ("x", f), rows[f].at[c, pl.ds(start, size)],
                rows[f].at[c, pl.ds(q * PLANE + start, size)], dev(dx=d), rows[f].at[c, pl.ds(PLANE, 2 * PLANE)],
            )

    def choose(p, f):
        if f == 0:
            matrices(p)
        arrive(("zb", p, f), tok[f].at[p, pl.ds(0, 5)])
        got = mm(pick[p], tok[f][p].reshape(NZ * PAD, WIDTHS[f])).astype(BF16)
        rows[f][c, base(p):base(p) + ROWS] = got[:ROWS]
        if p == 0:
            sideways(f, 0, ROWS)
        for d in (1, 2, 3):
            ysend[f][p, d - 1] = got[d * ROWS:(d + 1) * ROWS]
            send(
                ("y", p, f), ("y", p, f), ysend[f].at[p, d - 1],
                rows[f].at[c, pl.ds(base(p) + d * ROWS, ROWS)], dev(dy=d), ysend[f].at[p],
            )

    def to_sibling(f, start, size):
        block = rows[f].at[c, pl.ds(start, size)]
        send(("s", f), ("s", f), block, block, dev(dc=1), rows[f].at[c])

    def from_sibling(f):
        arrive(("s", f), rows[f].at[other])

    def onward(p, f):
        arrive(("y", p, f), rows[f].at[c, pl.ds(base(p) + ROWS, 3 * ROWS)])
        if p == 0:
            sideways(f, ROWS, PLANE - ROWS)
        to_sibling(f, base(p), PLANE)

    def neighbours(f):
        arrive(("x", f), rows[f].at[c, pl.ds(PLANE, 2 * PLANE)])
        to_sibling(f, PLANE, 2 * PLANE)

    def gate_up(f, h):
        depth = pl.ds(pl.multiple_of(h * half + STARTS[f], 128), WIDTHS[f])
        for q in range(2):
            block = rows[f][h, 2 * q * PLANE:2 * (q + 1) * PLANE]
            mine = pl.ds(2 * q * PLANE, 2 * PLANE)
            acc[mine, :HID] += mm(block, wg[depth, :])
            acc[mine, HID:] += mm(block, wu[depth, :])

    items = [(p, f) for p in range(2) for f in range(NF)]
    near(*items[0])
    send(("o", 0), ("om", 0), tm.at[0, 0], tm.at[1, 0], dev(dx=2), tm.at[0, 0])
    padded(1)
    near(*items[1])
    for f in range(NF):
        if f > 1:
            padded(f)
        send(("oz",), ("oz",), tok[f].at[0, 0], tok[f].at[1, 0], dev(dx=2), out)
    for load in loads:
        load.start()
    for f in range(NF):
        theirs = pl.ds(pl.multiple_of(other * half + STARTS[f], 128), WIDTHS[f])
        send(("w",), ("w",), wd_hbm.at[0, :, theirs], wd[f].at[pl.ds(HID, HID)], dev(dc=1), narrow)
    acc[...] = jnp.zeros_like(acc)

    def further(step):
        if step < len(items):
            far(*items[step])
        for later in {0: (2,), 1: (3, 4)}.get(step, (step + 3,)):
            if later < len(items):
                p, f = items[later]
                if p == 1:
                    if f == 0:
                        arrive(("om", 0), tm.at[0, 0])
                        arrive(("oz",), out)
                near(p, f)

    further(0)
    further(1)
    for step in range(len(items) + 2):
        if step < len(items):
            if step > 0:
                further(step + 2)
            choose(*items[step])
            if step == 0:
                further(2)
        if step >= 2:
            p, f = items[step - 2]
            if p == 1:
                sent([("z", 0, f), ("y", 0, f)])
            onward(p, f)
            if p == 1:
                neighbours(f)
                if f == 0:
                    loads[0].wait()
                    loads[1].wait()
                gate_up(f, c)
                if f > 0:
                    from_sibling(f - 1)
                    gate_up(f - 1, other)
    sent([key for key in outward if key != ("s", NF - 1)])
    from_sibling(NF - 1)
    gate_up(NF - 1, other)
    inner, outer = pl.ds(PLANE, 2 * PLANE), pl.ds(3 * PLANE, PLANE)
    first = pl.ds(0, PLANE)
    ours, theirs = pl.ds(0, HID), pl.ds(HID, HID)
    for key, mine in (("inner", inner), ("edge", outer), ("edge", first)):
        gate = acc[mine, :HID]
        hid[mine, ours] = (gate / (1.0 + jnp.exp(-gate)) * acc[mine, HID:]).astype(BF16)
        send(("h",), ("h", key), hid.at[mine, ours], hid.at[mine, theirs], dev(dc=1), hid.at[:, ours])

    sent([key for key in outward if key != ("h",)])
    pltpu.make_async_copy(narrow, narrow, wsem.at[2]).wait()
    arrive(("w",), narrow)
    arrive(("h", "inner"), hid.at[inner, theirs])

    def down(f, mine):
        part[f][mine] = mm(hid[mine], wd[f][...]).astype(BF16)

    def leave(f):
        down(f, inner)
        for d, q, place in ((-1, 1, 1), (1, 2, 0)):
            send(
                ("xb", f), ("xb", f), part[f].at[pl.ds(q * PLANE, PLANE)], xback[f].at[place], dev(dx=d), xback[f]
            )

    def leave_opposite(f):
        if f == 0:
            arrive(("h", "edge"), hid.at[inner, theirs])
        down(f, outer)
        down(f, first)

    def back(p, f):
        for d in (1, 2, 3):
            send(
                ("yb", p, f), ("yb", p, f), part[f].at[pl.ds(base(p) + d * ROWS, ROWS)],
                yback[f].at[p, pl.ds((d - 1) * ROWS, ROWS)], dev(dy=-d), yback[f].at[p],
            )

    def home(f):
        arrive(("xb", f), xback[f])
        total = part[f][first].astype(F32) + xback[f][0].astype(F32) + xback[f][1].astype(F32)
        part[f][first] = total.astype(BF16)
        back(0, f)

    def combine(p, f):
        arrive(("yb", p, f), yback[f].at[p])
        total = mm(mix[p, :, :ROWS], part[f][base(p):base(p) + ROWS])
        total += mm(mix[p, :, ROWS:], yback[f][p])
        zpart[f][p] = total.astype(BF16).reshape(NZ, PAD, WIDTHS[f])
        if (p, f) == (0, NF - 1):
            for j in range(1, NZ):
                send(("zi", p, f), ("zi", p, f), zpart[f].at[p, j], zlast.at[j - 1], dev(dz=-j), zlast)
            return
        for s, j, place in ((-1, 3, 0), (1, 5, 1), (-2 if f % 2 == 0 else 2, 4, 2)):
            send(("zi", p, f), ("zi", p, f), zpart[f].at[p, j], zfar[f].at[p, place], dev(dz=s), zfar[f].at[p])

    def closer(p, f):
        def home_by(s, j, place):
            send(("zn", p, f), ("zn", p, f), zpart[f].at[p, j], znear[f].at[p, place], dev(dz=s), znear[f].at[p])

        home_by(-1, 1, 0)
        home_by(1, 7, 1)
        arrive(("zi", p, f), zfar[f].at[p])
        two = zpart[f][p, 2].astype(F32) + zfar[f][p, 0].astype(F32)
        six = zpart[f][p, 6].astype(F32) + zfar[f][p, 1].astype(F32)
        if f % 2 == 0:
            two += zfar[f][p, 2].astype(F32)
        else:
            six += zfar[f][p, 2].astype(F32)
        zpart[f][p, 2] = two.astype(BF16)
        zpart[f][p, 6] = six.astype(BF16)
        home_by(-2, 2, 2)
        home_by(2, 6, 3)

    def gathered(p, f):
        arrive(("zn", p, f), znear[f].at[p])
        total = zpart[f][p, 0].astype(F32)
        for i in range(4):
            total += znear[f][p, i].astype(F32)
        return total

    def opposite(f):
        opp[f][0] = gathered(1, f).astype(BF16)
        send(("ob", f), ("ob", f), opp[f].at[0], opp[f].at[1], dev(dx=2), opp[f].at[0])

    def finish(f):
        if f < NF - 1:
            total = gathered(0, f)
        else:
            arrive(("zi", 0, f), zlast)
            total = zpart[f][0, 0].astype(F32)
            for i in range(NZ - 1):
                total += zlast[i].astype(F32)
        arrive(("ob", f), opp[f].at[0])
        total += opp[f][1].astype(F32)
        mine = pl.ds(STARTS[f], WIDTHS[f])
        out[:, mine] = total.astype(BF16)

    leave(0)
    leave(1)
    leave_opposite(0)
    leave(2)
    back(1, 0)
    leave(3)
    leave_opposite(1)
    back(1, 1)
    leave_opposite(3)
    leave_opposite(2)
    leave(4)
    back(1, 2)
    combine(1, 0)
    leave(5)
    back(1, 3)
    home(0)
    leave_opposite(5)
    combine(1, 1)
    combine(1, 2)
    closer(1, 1)
    closer(1, 0)
    home(1)
    combine(1, 3)
    back(1, 5)
    closer(1, 2)
    combine(0, 0)
    home(2)
    closer(1, 3)
    leave_opposite(4)
    back(1, 4)
    combine(1, 5)
    opposite(2)
    combine(0, 1)
    home(3)
    combine(0, 2)
    closer(0, 0)
    combine(1, 4)
    closer(0, 1)
    home(4)
    closer(1, 5)
    opposite(0)
    closer(0, 2)
    home(5)
    opposite(1)
    combine(0, 3)
    closer(1, 4)
    combine(0, 4)
    finish(0)
    opposite(3)
    opposite(5)
    combine(0, 5)
    finish(1)
    closer(0, 3)
    finish(2)
    closer(0, 4)
    opposite(4)
    finish(3)
    finish(5)
    finish(4)
    sent(list(outward))


def per_device(tokens, routes, route_weights, w_gate, w_up, w_down):
    half = tokens.shape[1]
    hbm = pl.BlockSpec(memory_space=pl.ANY)

    def chunked(*lead):
        return [pltpu.VMEM((*lead, width), BF16) for width in WIDTHS]

    result = pl.pallas_call(
        kernel,
        out_shape=pltpu.VMEM((PAD, half), BF16),
        in_specs=[hbm] * 6,
        out_specs=pl.BlockSpec(memory_space=pltpu.VMEM),
        scratch_shapes=[
            pltpu.VMEM((TOK, half), BF16),
            pltpu.VMEM((TOP, TOK), jnp.int32),
            pltpu.VMEM((TOP, TOK), F32),
            chunked(2, NZ, PAD),
            pltpu.VMEM((2, NZ, PAD, COLS), BF16),
            pltpu.VMEM((2, PLANE, NZ * PAD), BF16),
            pltpu.VMEM((2, NZ * PAD, PLANE), BF16),
            chunked(2, 3, ROWS),
            chunked(2, 4 * PLANE),
            pltpu.VMEM((2 * half, HID), BF16),
            pltpu.VMEM((2 * half, HID), BF16),
            chunked(2 * HID),
            pltpu.VMEM((4 * PLANE, 2 * HID), F32),
            pltpu.VMEM((4 * PLANE, 2 * HID), BF16),
            chunked(4 * PLANE),
            chunked(2, PLANE),
            chunked(2, 3 * ROWS),
            chunked(2, NZ, PAD),
            chunked(2, 3, PAD),
            chunked(2, 4, PAD),
            pltpu.VMEM((NZ - 1, PAD, WIDTHS[-1]), BF16),
            chunked(2, PAD),
            pltpu.SemaphoreType.DMA((3,)),
            pltpu.SemaphoreType.DMA((3,)),
            pltpu.SemaphoreType.DMA((48,)),
            pltpu.SemaphoreType.DMA((104,)),
        ],
        compiler_params=pltpu.CompilerParams(
            collective_id=0, has_side_effects=True, vmem_limit_bytes=60 * 1024 * 1024
        ),
        name="experts",
    )(tokens, routes.T, route_weights.T, w_gate, w_up, w_down)
    return result[:TOK]


def solution(mesh):
    placed = (
        P(("attn", "exp"), "rep"),
        P(("attn", "exp"), None),
        P(("attn", "exp"), None),
        P("exp", None, ("attn", "rep")),
        P("exp", None, ("attn", "rep")),
        P("exp", ("attn", "rep"), None),
    )
    return jax.shard_map(
        per_device, mesh=mesh, in_specs=placed, out_specs=P(("attn", "exp"), "rep"), check_vma=False
    )
```
